32 devices in a mesh: pts: 8 (over z, x), comp: 4 (over y, core).
Axes of the slice: x: 2, y: 2, z: 4, core: 2. Of those that a mesh axis runs over, the one named last changes fastest.
Arguments:
- points: bfloat16 [4096, 3072], P(('pts', 'comp')), may hold values from -6 to 6
- candidates: int32 [4096, 4], P(('pts', 'comp')), may hold values from 0 to 7, all different within a row; in each aligned block of 128 rows (0 to 127, 128 to 255, ...) at most 128 rows name the same one
- means: bfloat16 [1024, 3072], P('comp'), may hold values from -0.75 to 0.75
- variances: float32 [1024], P('comp'), may hold values from 0.9 to 1.1
- log_weights: float32 [1024], P('comp'), may hold values from -4 to 4
Outputs:
- loglik: float32 [4096], P(('pts', 'comp'))
- new_means: float32 [4, 256, 3072], P('comp', 'pts')
- new_variances: float32 [4, 256], P('comp', 'pts')
- new_log_weights: float32 [4, 256], P('comp', 'pts')
The draws below stay inside these ranges and needn't reach their ends.
Inputs may be any that keep to these rules, and one draw needn't show every extreme that they name: `candidates`: each row names 4 different blocks. Among the 128 rows of one device, no block is named by more than 128 rows, and some block is named by exactly 128 rows.
All inputs are finite; a program needn't handle non-finite values.
Results may differ from the reference program's by a relative error of at most 0.0065.
Values may be sent and summed in bfloat16 or wider, within the bound.
A program may use at most 64 MiB of HBM per device.

```python
import math
import jax
import jax.numpy as jnp
import numpy as np
from jax import lax

D = 3072
BLOCK = 128
CANDS = 4
PTS_DEV = 128
KDEV = 256
K = 1024
NBLK = 8
CAP = 128
NPTS = 4096
N_PTS = 8
N_COMP = 4


def shard_levels(stream_key, extent, pieces, smallest, top_value):
    gain, own = 1.0, jax.random.fold_in(stream_key, 6)
    for position, shards_of in pieces:
        heights = jnp.exp(jax.random.uniform(jax.random.fold_in(own, position), (shards_of,), jnp.float32, smallest / len(pieces), top_value / len(pieces)))
        gain = gain * jnp.repeat(heights, extent[position] // shards_of).reshape([-1 if axis == position else 1 for axis in range(len(extent))])
    return gain


def deal_out(key, own, number, rows, number_of, top, reach, lean):
    order = jax.random.permutation(key, number_of)
    heavy_load, usual = portions_of(number_of, rows * top, reach, lean, True), portions_of(number_of, rows * top, reach, lean, False)
    places = jnp.arange(number_of)

    def named(lengths, turn):
        used = int((lengths > 0).sum())
        fixed = max(1, used // 4)
        moved = fixed + (places - fixed + turn * (used - fixed)) % max(1, number_of - fixed)
        return jnp.zeros((number_of,), jnp.int32).at[order[jnp.where(places < fixed, places, moved)]].set(jnp.asarray(lengths, jnp.int32))

    lengths = jnp.where(number % 4 == 0, named(heavy_load, number // 4), named(usual, number - number // 4 - 1))
    mixed = jax.random.permutation(jax.random.fold_in(own, 3), number_of)
    donor, sink = mixed[0:number_of // 2 * 2:2], mixed[1:number_of // 2 * 2:2]
    margin = jnp.minimum(lengths[donor] - 1, reach - lengths[sink]) // 2
    margin = jnp.where((donor == order[0]) | (sink == order[0]) | (lengths[sink] == 0), 0, jnp.maximum(margin, 0))
    moved = jax.random.randint(jax.random.fold_in(own, 4), (number_of // 2,), 0, 1 << 20) % (margin + 1)
    lengths = lengths.at[donor].add(-moved).at[sink].add(moved)
    members = jnp.searchsorted(jnp.cumsum(lengths), jnp.arange(rows * top), side="right").astype(jnp.int32)
    listing = members.reshape(top, rows).T
    listing = listing[jax.random.permutation(jax.random.fold_in(own, 1), rows)]
    turn = jax.random.randint(jax.random.fold_in(own, 2), (rows, 1), 0, top)
    return jnp.take_along_axis(listing, (jnp.arange(top)[None, :] + turn) % top, axis=1)


def portions_of(count, total, bound, lean, full):
    weights = [(1 << 20) // math.isqrt(standing ** lean) + 1 for standing in range(1, count + 1)]
    largest = bound if full else min(bound, max(-(-total // count), total * weights[0] // sum(weights)))
    least = 1 if total - largest >= count - 1 else 0
    given, surplus = [largest] + [least] * (count - 1), total - largest - least * (count - 1)
    while surplus > 0:
        movable = [i for i in range(1, count) if given[i] < largest] or [i for i in range(1, count) if given[i] < bound]
        whole, left = sum([weights[i] for i in movable]), surplus
        for i in movable:
            addition = min(bound - given[i], max(1, left * weights[i] // whole), surplus)
            given[i] = given[i] + addition
            surplus = surplus - addition
    return np.array(given)


def scatter_about(stream_key, dims, deviation, limit, pieces=(), held_as=jnp.bfloat16):
    result = deviation * jax.random.normal(stream_key, dims, jnp.float32)
    if pieces:
        result = result * shard_levels(stream_key, dims, pieces, -0.22, 0.18)
    return jnp.clip(result, -limit, limit).astype(held_as)


def setup_inputs(seed: int = 0) -> dict:
    keys = jax.random.split(jax.random.key(seed), 6)
    points = scatter_about(keys[0], (NPTS, D), 1.0, 6.0, ((0, 32),))
    candidates_keys = jax.random.split(jax.random.fold_in(keys[1], 1), NPTS // PTS_DEV)
    candidates_turns = jax.random.permutation(jax.random.fold_in(keys[1], 3), NPTS // PTS_DEV)
    candidates = jax.vmap(lambda own, number: deal_out(jax.random.fold_in(keys[1], 2), own, number, PTS_DEV, NBLK, CANDS, CAP, 2))(candidates_keys, candidates_turns).reshape((NPTS, CANDS))
    means = scatter_about(keys[2], (K, D), 0.05, 0.75, ((0, 4),))
    variances = jnp.clip(1.0 + 0.02 * jax.random.normal(keys[3], (K,), jnp.float32), 0.9, 1.1)
    log_weights = scatter_about(keys[4], (K,), 1.0, 4.0, ((0, 4),), jnp.float32)
    return {"points": points, "candidates": candidates, "means": means, "variances": variances, "log_weights": log_weights}


def log_density(rows, mu, var, logw):
    rows32 = rows.astype(jnp.float32)
    mu32 = mu.astype(jnp.float32)
    inner = jnp.dot(rows32, mu32.T, precision=lax.Precision.HIGHEST)
    xx = jnp.sum(rows32 * rows32, axis=1)
    mm = jnp.sum(mu32 * mu32, axis=1)
    const = logw - 0.5 * D * jnp.log(2.0 * math.pi * var)
    return const[None, :] - (xx[:, None] - 2.0 * inner + mm[None, :]) / (2.0 * var[None, :]), xx


def reference(points, candidates, means, variances, log_weights):
    npair = NPTS * CANDS
    padb = CAP * N_PTS * N_COMP
    flat = candidates.reshape(-1)
    seq = jnp.arange(npair, dtype=jnp.int32)
    order = jnp.argsort(flat * npair + seq).astype(jnp.int32)
    counts_blk = jnp.sum((flat[:, None] == jnp.arange(NBLK, dtype=jnp.int32)[None, :]).astype(jnp.int32), axis=0)
    starts = (jnp.cumsum(counts_blk) - counts_blk).astype(jnp.int32)
    order_pad = jnp.concatenate([order, jnp.full((padb,), npair, jnp.int32)])

    def block_data(b):
        idx = lax.dynamic_slice_in_dim(order_pad, starts[b], padb)
        valid = jnp.arange(padb, dtype=jnp.int32) < counts_blk[b]
        pair = jnp.where(valid, idx, 0).astype(jnp.int32)
        rows = points[pair // CANDS]
        mu = lax.dynamic_slice_in_dim(means, b * BLOCK, BLOCK)
        var = lax.dynamic_slice_in_dim(variances, b * BLOCK, BLOCK)
        logw = lax.dynamic_slice_in_dim(log_weights, b * BLOCK, BLOCK)
        logp, xx = log_density(rows, mu, var, logw)
        return pair, valid, rows, logp, xx

    def first(b):
        pair, valid, rows, logp, xx = block_data(b)
        bmax = jnp.max(logp, axis=1)
        bsum = jnp.sum(jnp.exp(logp - bmax[:, None]), axis=1)
        return jnp.where(valid, pair, npair), bmax, bsum

    blocks = jnp.arange(NBLK, dtype=jnp.int32)
    target, bmax, bsum = lax.map(first, blocks)
    target = target.reshape(-1)
    pmax = jnp.zeros((npair + 1,), jnp.float32).at[target].set(bmax.reshape(-1))[:npair].reshape(NPTS, CANDS)
    psum = jnp.zeros((npair + 1,), jnp.float32).at[target].set(bsum.reshape(-1))[:npair].reshape(NPTS, CANDS)
    top = jnp.max(pmax, axis=1)
    loglik = top + jnp.log(jnp.sum(psum * jnp.exp(pmax - top[:, None]), axis=1))

    def second(b):
        pair, valid, rows, logp, xx = block_data(b)
        resp = jnp.exp(logp - loglik[pair // CANDS][:, None])
        resp = jnp.where(valid[:, None], resp, 0.0)
        counts = jnp.sum(resp, axis=0)
        sqsum = jnp.sum(resp * xx[:, None], axis=0)
        resp16 = resp.astype(jnp.bfloat16).astype(jnp.float32)
        wsum = jnp.dot(resp16.T, rows.astype(jnp.float32), precision=lax.Precision.HIGHEST)
        return counts, sqsum, wsum

    counts, sqsum, wsum = lax.map(second, blocks)
    counts = counts.reshape(K)
    sqsum = sqsum.reshape(K)
    wsum = wsum.reshape(K, D)
    mu_old = means.astype(jnp.float32)
    new_means = (wsum + mu_old) / (counts + 1.0)[:, None]
    resid = sqsum - 2.0 * jnp.sum(new_means * wsum, axis=1) + counts * jnp.sum(new_means * new_means, axis=1) + D * variances
    new_variances = resid / (D * (counts + 1.0))
    new_log_weights = jnp.log((counts + 1.0) / float(NPTS + K))
    return loglik, new_means.reshape(N_COMP, KDEV, D), new_variances.reshape(N_COMP, KDEV), new_log_weights.reshape(N_COMP, KDEV)
```

```python
import functools
import math

import jax
import jax.numpy as jnp
from jax import lax
from jax.experimental import pallas as pl
from jax.experimental.pallas import tpu as pltpu
from jax.sharding import PartitionSpec as P

MESH = pl.DeviceIdType.MESH
LANES = 128
LOW = -3.0e38


def em_kernel(
    ncomp, npts, inner, pieces,
    points_ref, cand_ref, means_ref, shares_ref, var_ref, logw_ref,
    loglik_ref, mean_ref, newvar_ref, newlogw_ref,
    gathered, means, mu_old, aux, logp, stats, logliks, resp16, sums,
    wsend, wrecv, relay, wland, wtotal,
    load_sem, y_send, y_recv, sib_send, sib_recv, fwd_send, fwd_recv,
    aux_send, aux_recv, st_send, st_recv, sum_send, sum_recv,
    w_send, w_recv, g_send, g_recv,
):
    here_c, here_p = lax.axis_index("comp"), lax.axis_index("pts")
    ny, ngroups = ncomp // 2, npts // inner
    rows, width = points_ref.shape
    owned = means_ref.shape[0]
    block = owned // 2
    share = owned // npts
    piece = width // pieces
    y, core = here_c // 2, here_c % 2
    other_core = 1 - core
    sibling = y * 2 + other_core
    group, place = here_p // inner, here_p % inner

    load_points = pltpu.make_async_copy(points_ref, gathered.at[here_c], load_sem.at[0])
    load_points.start()
    load_means = pltpu.make_async_copy(means_ref, means, load_sem.at[1])
    load_means.start()
    load_share = pltpu.make_async_copy(shares_ref.at[here_p], mu_old, load_sem.at[2])
    load_share.start()

    barrier = pltpu.get_barrier_semaphore()
    for k in range(1, ncomp):
        pl.semaphore_signal(
            barrier, inc=1, device_id=(here_p, (here_c + k) % ncomp), device_id_type=MESH
        )
    for k in range(1, npts):
        pl.semaphore_signal(
            barrier, inc=1, device_id=((here_p + k) % npts, here_c), device_id_type=MESH
        )
    load_points.wait()
    pl.semaphore_wait(barrier, ncomp + npts - 2)

    sends = []

    def send(src, dst, s_sem, r_sem, device):
        copy = pltpu.make_async_remote_copy(
            src_ref=src, dst_ref=dst, send_sem=s_sem, recv_sem=r_sem,
            device_id=device, device_id_type=MESH,
        )
        copy.start()
        sends.append(copy)

    def arrived(dst, s_sem, r_sem):
        pltpu.make_async_remote_copy(
            src_ref=dst, dst_ref=dst, send_sem=s_sem, recv_sem=r_sem,
            device_id=(here_p, sibling), device_id_type=MESH,
        ).wait_recv()

    def part(slot, c):
        return gathered.at[slot, :, pl.ds(c * piece, piece)]

    for c in range(pieces):
        for k in range(1, ny):
            send(part(here_c, c), part(here_c, c), y_send.at[k - 1, c], y_recv.at[k - 1, c],
                 (here_p, ((y + k) % ny) * 2 + core))
        send(part(here_c, c), part(here_c, c), sib_send.at[c], sib_recv.at[c], (here_p, sibling))

    def add_square(ref):
        def body(j, total):
            x = ref[:, pl.ds(pl.multiple_of(j * LANES, LANES), LANES)].astype(jnp.float32)
            return total + x * x
        return body

    own_points = gathered.at[here_c]
    sq = lax.fori_loop(
        0, width // LANES, add_square(own_points), jnp.zeros((rows, LANES), jnp.float32)
    )
    xx_row = jnp.sum(sq.T, axis=0, keepdims=True)
    ncand = cand_ref.shape[1]
    eye = lax.broadcasted_iota(jnp.int32, (rows, rows), 0) == lax.broadcasted_iota(
        jnp.int32, (rows, rows), 1
    )
    cand = cand_ref[...].astype(jnp.float32)
    cand_rows = [
        jnp.sum(jnp.where(eye, cand[:, j : j + 1], 0.0), axis=0, keepdims=True)
        for j in range(ncand)
    ]
    aux[here_c] = jnp.concatenate(
        cand_rows + [xx_row] + [jnp.zeros((aux.shape[1] - ncand - 1, rows), jnp.float32)], axis=0
    )
    for k in range(1, ncomp):
        send(aux.at[here_c], aux.at[here_c], aux_send.at[k - 1], aux_recv.at[k - 1],
             (here_p, (here_c + k) % ncomp))

    load_means.wait()

    def dot_t(slot, lo, size):
        return lax.dot_general(
            means[:, pl.ds(lo, size)], gathered[slot, :, pl.ds(lo, size)],
            (((1,), (1,)), ((), ())), preferred_element_type=jnp.float32,
        )

    logp[here_c] = dot_t(here_c, 0, width)

    sq = lax.fori_loop(
        0, width // LANES, add_square(means), jnp.zeros((owned, LANES), jnp.float32)
    )
    mm = jnp.sum(sq, axis=1, keepdims=True)
    eye_k = lax.broadcasted_iota(jnp.int32, (owned, owned), 0) == lax.broadcasted_iota(
        jnp.int32, (owned, owned), 1
    )
    var = jnp.sum(jnp.where(eye_k, var_ref[...], 0.0), axis=1, keepdims=True)
    logw = jnp.sum(jnp.where(eye_k, logw_ref[...], 0.0), axis=1, keepdims=True)
    const = logw - 0.5 * width * jnp.log(2.0 * math.pi * var)
    two_var = 2.0 * var

    for c in range(pieces):
        arrived(part(sibling, c), sib_send.at[c], sib_recv.at[c])
    logp[sibling] = dot_t(sibling, 0, width)

    def accumulate(slot, c):
        term = dot_t(slot, c * piece, piece)
        logp[slot] = term if c == 0 else logp[slot] + term

    def take_forwarded(c):
        for k in range(1, ny):
            slot = ((y + ny - k) % ny) * 2 + other_core
            arrived(part(slot, c), fwd_send.at[k - 1, c], fwd_recv.at[k - 1, c])
            accumulate(slot, c)

    for c in range(pieces):
        for k in range(1, ny):
            slot = ((y + ny - k) % ny) * 2 + core
            arrived(part(slot, c), y_send.at[k - 1, c], y_recv.at[k - 1, c])
            send(part(slot, c), part(slot, c), fwd_send.at[k - 1, c], fwd_recv.at[k - 1, c],
                 (here_p, sibling))
            accumulate(slot, c)
        if c:
            take_forwarded(c - 1)
    take_forwarded(pieces - 1)
    for k in range(1, ncomp):
        arrived(aux.at[(here_c + ncomp - k) % ncomp], aux_send.at[k - 1], aux_recv.at[k - 1])

    def named(s, b):
        number = (here_c * 2 + b).astype(jnp.float32)
        hit = aux[s, 0:1, :] == number
        for j in range(1, ncand):
            hit = hit | (aux[s, j : j + 1, :] == number)
        return hit

    for s in range(ncomp):
        xx = aux[s, ncand : ncand + 1, :]
        lp = const - (xx - 2.0 * logp[s] + mm) / two_var
        logp[s] = lp
        tops, totals = [], []
        for b in range(2):
            half = lp[b * block : (b + 1) * block]
            top = jnp.max(half, axis=0, keepdims=True)
            total = jnp.sum(jnp.exp(half - top), axis=0, keepdims=True)
            hit = named(s, b)
            tops.append(jnp.where(hit, top, LOW))
            totals.append(jnp.where(hit, total, 0.0))
        top = jnp.maximum(tops[0], tops[1])
        total = totals[0] * jnp.exp(tops[0] - top) + totals[1] * jnp.exp(tops[1] - top)
        stats[here_c, 0:1, s * rows : (s + 1) * rows] = top
        stats[here_c, 1:2, s * rows : (s + 1) * rows] = total
    for k in range(1, ncomp):
        send(stats.at[here_c], stats.at[here_c], st_send.at[k - 1], st_recv.at[k - 1],
             (here_p, (here_c + k) % ncomp))
    for k in range(1, ncomp):
        arrived(stats.at[(here_c + ncomp - k) % ncomp], st_send.at[k - 1], st_recv.at[k - 1])

    count_sum = [jnp.zeros((block, rows), jnp.float32) for _ in range(2)]
    sq_sum = [jnp.zeros((block, rows), jnp.float32) for _ in range(2)]
    for s in range(ncomp):
        lanes = slice(s * rows, (s + 1) * rows)
        tops = [stats[o, 0:1, lanes] for o in range(ncomp)]
        top = functools.reduce(jnp.maximum, tops)
        total = stats[0, 1:2, lanes] * jnp.exp(tops[0] - top)
        for o in range(1, ncomp):
            total = total + stats[o, 1:2, lanes] * jnp.exp(tops[o] - top)
        loglik = top + jnp.log(total)
        logliks[s] = loglik
        xx = aux[s, ncand : ncand + 1, :]
        for b in range(2):
            resp = jnp.where(
                named(s, b), jnp.exp(logp[s, b * block : (b + 1) * block, :] - loglik), 0.0
            )
            resp16[b * block : (b + 1) * block, lanes] = resp.astype(jnp.bfloat16)
            count_sum[b] = count_sum[b] + resp
            sq_sum[b] = sq_sum[b] + resp * xx
    loglik_ref[...] = logliks[here_c]
    for b in range(2):
        cols = slice(b * block, (b + 1) * block)
        sums[0, 0:1, cols] = jnp.sum(count_sum[b].T, axis=0, keepdims=True)
        sums[0, 1:2, cols] = jnp.sum(sq_sum[b].T, axis=0, keepdims=True)
    for k in range(1, npts):
        send(sums.at[0], sums.at[k], sum_send.at[k - 1], sum_recv.at[k - 1],
             ((here_p + k) % npts, here_c))

    for c in range(pieces):
        cols = pl.ds(c * piece, piece)
        data = gathered[:, :, cols].reshape(ncomp * rows, piece)
        w = jnp.dot(resp16[...], data, preferred_element_type=jnp.float32)
        for g in range(ngroups):
            for i in range(inner):
                first = (g * inner + i) * share
                wsend[i, g, :, cols] = w[first : first + share].astype(jnp.bfloat16)
        for k in range(1, inner):
            to = (place + k) % inner
            send(wsend.at[to, :, :, cols], wrecv.at[k - 1, :, :, cols],
                 w_send.at[k - 1, c], w_recv.at[k - 1, c], (group * inner + to, here_c))

    for c in range(pieces):
        cols = pl.ds(c * piece, piece)
        total = wsend[place, :, :, cols].astype(jnp.float32)
        for k in range(1, inner):
            arrived(wrecv.at[k - 1, :, :, cols], w_send.at[k - 1, c], w_recv.at[k - 1, c])
            total = total + wrecv[k - 1, :, :, cols].astype(jnp.float32)
        wtotal[:, :, cols] = total
        relay[:, :, cols] = total.astype(jnp.bfloat16)
        for k in range(1, ngroups):
            to = (group + k) % ngroups
            send(relay.at[to, :, cols], wland.at[k - 1, :, cols],
                 g_send.at[k - 1, c], g_recv.at[k - 1, c], (to * inner + place, here_c))

    for k in range(1, npts):
        arrived(sums.at[k], sum_send.at[k - 1], sum_recv.at[k - 1])
    both = sums[0]
    for k in range(1, npts):
        both = both + sums[k]
    mine = lax.broadcasted_iota(jnp.int32, (share, owned), 1) == (
        lax.broadcasted_iota(jnp.int32, (share, owned), 0) + here_p * share
    )

    def column(row):
        return jnp.sum(jnp.where(mine, row, 0.0), axis=1, keepdims=True)

    counts, sqsum, var_old = column(both[0:1]), column(both[1:2]), column(var_ref[...])
    load_share.wait()
    cross = jnp.zeros((share, 1), jnp.float32)
    norm = jnp.zeros((share, 1), jnp.float32)
    for c in range(pieces):
        cols = pl.ds(c * piece, piece)
        w = wtotal[group, :, cols]
        for k in range(1, ngroups):
            arrived(wland.at[k - 1, :, cols], g_send.at[k - 1, c], g_recv.at[k - 1, c])
            w = w + wland[k - 1, :, cols].astype(jnp.float32)
        new = (w + mu_old[:, cols].astype(jnp.float32)) / (counts + 1.0)
        mean_ref[:, cols] = new
        cross = cross + jnp.sum(new * w, axis=1, keepdims=True)
        norm = norm + jnp.sum(new * new, axis=1, keepdims=True)
    resid = sqsum - 2.0 * cross + counts * norm + width * var_old
    new_var = resid / (width * (counts + 1.0))
    new_logw = jnp.log((counts + 1.0) / float(rows * ncomp * npts + owned * ncomp))
    eye_s = lax.broadcasted_iota(jnp.int32, (share, share), 0) == lax.broadcasted_iota(
        jnp.int32, (share, share), 1
    )
    newvar_ref[...] = jnp.sum(jnp.where(eye_s, new_var, 0.0), axis=0, keepdims=True)
    newlogw_ref[...] = jnp.sum(jnp.where(eye_s, new_logw, 0.0), axis=0, keepdims=True)

    for copy in sends:
        copy.wait_send()


def on_device(ncomp, npts, points, candidates, means, variances, log_weights):
    rows, width = points.shape
    owned = means.shape[0]
    share = owned // npts
    inner = 2 ** (npts.bit_length() // 2)
    ngroups = npts // inner
    pieces = 4
    ny = ncomp // 2
    aux_rows = -(-(candidates.shape[1] + 1) // 8) * 8
    f32, bf16 = jnp.float32, jnp.bfloat16
    dma = pltpu.SemaphoreType.DMA
    vmem = pl.BlockSpec(memory_space=pltpu.VMEM)
    anywhere = pl.BlockSpec(memory_space=pl.ANY)
    loglik, new_means, new_var, new_logw = pl.pallas_call(
        functools.partial(em_kernel, ncomp, npts, inner, pieces),
        out_shape=(
            jax.ShapeDtypeStruct((1, rows), f32),
            jax.ShapeDtypeStruct((share, width), f32),
            jax.ShapeDtypeStruct((1, share), f32),
            jax.ShapeDtypeStruct((1, share), f32),
        ),
        in_specs=[anywhere, vmem, anywhere, anywhere, vmem, vmem],
        out_specs=(vmem, vmem, vmem, vmem),
        scratch_shapes=[
            pltpu.VMEM((ncomp, rows, width), bf16),
            pltpu.VMEM((owned, width), bf16),
            pltpu.VMEM((share, width), bf16),
            pltpu.VMEM((ncomp, aux_rows, rows), f32),
            pltpu.VMEM((ncomp, owned, rows), f32),
            pltpu.VMEM((ncomp, 2, ncomp * rows), f32),
            pltpu.VMEM((ncomp, 1, rows), f32),
            pltpu.VMEM((owned, ncomp * rows), bf16),
            pltpu.VMEM((npts, 2, owned), f32),
            pltpu.VMEM((inner, ngroups, share, width), bf16),
            pltpu.VMEM((inner - 1, ngroups, share, width), bf16),
            pltpu.VMEM((ngroups, share, width), bf16),
            pltpu.VMEM((ngroups - 1, share, width), bf16),
            pltpu.VMEM((ngroups, share, width), f32),
            dma((3,)),
            dma((ny - 1, pieces)), dma((ny - 1, pieces)),
            dma((pieces,)), dma((pieces,)),
            dma((ny - 1, pieces)), dma((ny - 1, pieces)),
            dma((ncomp - 1,)), dma((ncomp - 1,)),
            dma((ncomp - 1,)), dma((ncomp - 1,)),
            dma((npts - 1,)), dma((npts - 1,)),
            dma((inner - 1, pieces)), dma((inner - 1, pieces)),
            dma((ngroups - 1, pieces)), dma((ngroups - 1, pieces)),
        ],
        compiler_params=pltpu.CompilerParams(
            collective_id=0, has_side_effects=True, vmem_limit_bytes=50 * 1024 * 1024
        ),
        name="em_step",
    )(
        points, candidates, means, means.reshape(npts, share, width),
        variances.reshape(1, owned), log_weights.reshape(1, owned),
    )
    return (
        loglik.reshape(rows),
        new_means.reshape(1, share, width),
        new_var,
        new_logw,
    )


def solution(mesh):
    return jax.shard_map(
        functools.partial(on_device, mesh.shape["comp"], mesh.shape["pts"]),
        mesh=mesh,
        in_specs=(
            P(("pts", "comp"), None),
            P(("pts", "comp"), None),
            P("comp", None),
            P("comp"),
            P("comp"),
        ),
        out_specs=(P(("pts", "comp")), P("comp", "pts", None), P("comp", "pts"), P("comp", "pts")),
        check_vma=False,
    )
```

```python
import functools
import math

import jax
import jax.numpy as jnp
from jax import lax
from jax.experimental import pallas as pl
from jax.experimental.pallas import tpu as pltpu
from jax.sharding import PartitionSpec as P

MESH = pl.DeviceIdType.MESH
LANES = 128
LOW = -3.0e38


def em_kernel(
    ncomp, npts, pieces,
    points_ref, cand_ref, means_ref, shares_ref, var_ref, logw_ref,
    loglik_ref, mean_ref, newvar_ref, newlogw_ref,
    gathered, means, mu_old, cands, var_row, logw_row, aux, logp, stats, logliks, resp16, sums,
    wsend, land0, kept, relay1, land1, total, relay2, land2,
    load_sem, y_send, y_recv, sib_send, sib_recv, fwd_send, fwd_recv,
    aux_send, aux_recv, st_send, st_recv, sum_send, sum_recv,
    send0, recv0, send1, recv1, send2, recv2,
):
    here_c, here_p = lax.axis_index("comp"), lax.axis_index("pts")
    ny, ngroups = ncomp // 2, npts // 4
    rows, width = points_ref.shape
    owned = means_ref.shape[0]
    block = owned // 2
    share = owned // npts
    piece = width // pieces
    ncand = cand_ref.shape[0]
    y, core = here_c // 2, here_c % 2
    other_core = 1 - core
    sibling = y * 2 + other_core
    group = here_p // 4
    stride0, stride1 = 1 + core, 2 - core
    bit0, bit1 = (here_p // stride0) % 2, (here_p // stride1) % 2
    partner0 = here_p + (1 - 2 * bit0) * stride0
    partner1 = here_p + (1 - 2 * bit1) * stride1

    barrier = pltpu.get_barrier_semaphore()
    for k in range(1, ncomp):
        pl.semaphore_signal(
            barrier, inc=1, device_id=(here_p, (here_c + k) % ncomp), device_id_type=MESH
        )
    for k in range(1, npts):
        pl.semaphore_signal(
            barrier, inc=1, device_id=((here_p + k) % npts, here_c), device_id_type=MESH
        )

    loads = [
        pltpu.make_async_copy(src, dst, load_sem.at[i])
        for i, (src, dst) in enumerate(
            [
                (points_ref, gathered.at[here_c]), (cand_ref, cands), (means_ref, means),
                (var_ref, var_row), (logw_ref, logw_row), (shares_ref.at[here_p], mu_old),
            ]
        )
    ]
    for load in loads:
        load.start()

    def add_square(ref):
        def body(j, acc):
            x = ref[:, pl.ds(pl.multiple_of(j * LANES, LANES), LANES)].astype(jnp.float32)
            return acc + x * x
        return body

    loads[0].wait()
    loads[1].wait()
    sq = lax.fori_loop(
        0, width // LANES, add_square(gathered.at[here_c]), jnp.zeros((rows, LANES), jnp.float32)
    )
    xx_row = jnp.sum(sq.T, axis=0, keepdims=True)
    aux[here_c] = jnp.concatenate(
        [cands[...].astype(jnp.float32), xx_row]
        + [jnp.zeros((aux.shape[1] - ncand - 1, rows), jnp.float32)],
        axis=0,
    )
    pl.semaphore_wait(barrier, ncomp + npts - 2)

    sends = []

    def send(src, dst, s_sem, r_sem, device):
        copy = pltpu.make_async_remote_copy(
            src_ref=src, dst_ref=dst, send_sem=s_sem, recv_sem=r_sem,
            device_id=device, device_id_type=MESH,
        )
        copy.start()
        sends.append(copy)

    def arrived(dst, s_sem, r_sem):
        pltpu.make_async_remote_copy(
            src_ref=dst, dst_ref=dst, send_sem=s_sem, recv_sem=r_sem,
            device_id=(here_p, sibling), device_id_type=MESH,
        ).wait_recv()

    def part(slot, c):
        return gathered.at[slot, :, pl.ds(c * piece, piece)]

    for c in range(pieces):
        for k in range(1, ny):
            send(part(here_c, c), part(here_c, c), y_send.at[k - 1, c], y_recv.at[k - 1, c],
                 (here_p, ((y + k) % ny) * 2 + core))
        if c == 0:
            for k in range(1, ncomp):
                send(aux.at[here_c], aux.at[here_c], aux_send.at[k - 1], aux_recv.at[k - 1],
                     (here_p, (here_c + k) % ncomp))
    send(gathered.at[here_c], gathered.at[here_c], sib_send.at[0], sib_recv.at[0],
         (here_p, sibling))

    for load in loads[2:]:
        load.wait()

    def dot_t(slot, lo, size):
        return lax.dot_general(
            means[:, pl.ds(lo, size)], gathered[slot, :, pl.ds(lo, size)],
            (((1,), (1,)), ((), ())), preferred_element_type=jnp.float32,
        )

    sq = lax.fori_loop(
        0, width // LANES, add_square(means), jnp.zeros((owned, LANES), jnp.float32)
    )
    mm = jnp.sum(sq, axis=1, keepdims=True)
    eye_k = lax.broadcasted_iota(jnp.int32, (owned, owned), 0) == lax.broadcasted_iota(
        jnp.int32, (owned, owned), 1
    )
    var = jnp.sum(jnp.where(eye_k, var_row[...], 0.0), axis=1, keepdims=True)
    logw = jnp.sum(jnp.where(eye_k, logw_row[...], 0.0), axis=1, keepdims=True)
    const = logw - 0.5 * width * jnp.log(2.0 * math.pi * var)
    two_var = 2.0 * var

    def named(s, b):
        number = (here_c * 2 + b).astype(jnp.float32)
        hit = aux[s, 0:1, :] == number
        for j in range(1, ncand):
            hit = hit | (aux[s, j : j + 1, :] == number)
        return hit

    def finish(s, g):
        xx = aux[s, ncand : ncand + 1, :]
        lp = const - (xx - 2.0 * g + mm) / two_var
        logp[s] = lp
        tops, totals = [], []
        for b in range(2):
            half = lp[b * block : (b + 1) * block]
            top = jnp.max(half, axis=0, keepdims=True)
            hit = named(s, b)
            part_sum = jnp.sum(jnp.exp(half - top), axis=0, keepdims=True)
            tops.append(jnp.where(hit, top, LOW))
            totals.append(jnp.where(hit, part_sum, 0.0))
        top = jnp.maximum(tops[0], tops[1])
        stats[here_c, s, 0:1, :] = top
        stats[here_c, s, 1:2, :] = totals[0] * jnp.exp(tops[0] - top) + totals[1] * jnp.exp(
            tops[1] - top
        )
        for k in range(1, ncomp):
            send(stats.at[here_c, s], stats.at[here_c, s], st_send.at[k - 1, s],
                 st_recv.at[k - 1, s], (here_p, (here_c + k) % ncomp))

    finish(here_c, dot_t(here_c, 0, width))
    for k in range(1, ncomp):
        arrived(aux.at[(here_c + ncomp - k) % ncomp], aux_send.at[k - 1], aux_recv.at[k - 1])
    arrived(gathered.at[sibling], sib_send.at[0], sib_recv.at[0])
    finish(sibling, dot_t(sibling, 0, width))

    def accumulate(slot, c):
        g = dot_t(slot, c * piece, piece)
        if c:
            g = logp[slot] + g
        if c < pieces - 1:
            logp[slot] = g
        else:
            finish(slot, g)

    def take_forwarded(c):
        for k in range(1, ny):
            slot = ((y + ny - k) % ny) * 2 + other_core
            arrived(part(slot, c), fwd_send.at[k - 1, c], fwd_recv.at[k - 1, c])
            accumulate(slot, c)

    for c in range(pieces):
        for k in range(1, ny):
            slot = ((y + ny - k) % ny) * 2 + core
            arrived(part(slot, c), y_send.at[k - 1, c], y_recv.at[k - 1, c])
            send(part(slot, c), part(slot, c), fwd_send.at[k - 1, c], fwd_recv.at[k - 1, c],
                 (here_p, sibling))
            accumulate(slot, c)
        if c:
            take_forwarded(c - 1)
    take_forwarded(pieces - 1)

    for k in range(1, ncomp):
        owner = (here_c + ncomp - k) % ncomp
        for s in range(ncomp):
            arrived(stats.at[owner, s], st_send.at[k - 1, s], st_recv.at[k - 1, s])

    count_sum = [jnp.zeros((block, rows), jnp.float32) for _ in range(2)]
    sq_sum = [jnp.zeros((block, rows), jnp.float32) for _ in range(2)]
    for s in range(ncomp):
        lanes = slice(s * rows, (s + 1) * rows)
        tops = [stats[o, s, 0:1, :] for o in range(ncomp)]
        top = functools.reduce(jnp.maximum, tops)
        weight = stats[0, s, 1:2, :] * jnp.exp(tops[0] - top)
        for o in range(1, ncomp):
            weight = weight + stats[o, s, 1:2, :] * jnp.exp(tops[o] - top)
        loglik = top + jnp.log(weight)
        logliks[s] = loglik
        xx = aux[s, ncand : ncand + 1, :]
        for b in range(2):
            resp = jnp.where(
                named(s, b), jnp.exp(logp[s, b * block : (b + 1) * block, :] - loglik), 0.0
            )
            resp16[b * block : (b + 1) * block, lanes] = resp.astype(jnp.bfloat16)
            count_sum[b] = count_sum[b] + resp
            sq_sum[b] = sq_sum[b] + resp * xx

    def make(c):
        cols = pl.ds(c * piece, piece)
        data = gathered[:, :, cols].reshape(ncomp * rows, piece)
        w = jnp.dot(resp16[...], data, preferred_element_type=jnp.float32)
        for g in range(ngroups):
            for hi in range(2):
                for lo in range(2):
                    first = (g * 4 + hi * 2 + lo) * share
                    wsend[lo + core * (hi - lo), hi + core * (lo - hi), g, :, cols] = w[
                        first : first + share
                    ].astype(jnp.bfloat16)
        send(wsend.at[1 - bit0, :, :, :, cols], land0.at[:, :, :, cols],
             send0.at[c], recv0.at[c], (partner0, here_c))

    def halve(c):
        cols = pl.ds(c * piece, piece)
        arrived(land0.at[:, :, :, cols], send0.at[c], recv0.at[c])
        relay1[:, :, cols] = (
            wsend[bit0, 1 - bit1, :, :, cols].astype(jnp.float32)
            + land0[1 - bit1, :, :, cols].astype(jnp.float32)
        ).astype(jnp.bfloat16)
        send(relay1.at[:, :, cols], land1.at[:, :, cols], send1.at[c], recv1.at[c],
             (partner1, here_c))
        kept[:, :, cols] = wsend[bit0, bit1, :, :, cols].astype(jnp.float32) + land0[
            bit1, :, :, cols
        ].astype(jnp.float32)

    def spread(c):
        cols = pl.ds(c * piece, piece)
        arrived(land1.at[:, :, cols], send1.at[c], recv1.at[c])
        both = kept[:, :, cols] + land1[:, :, cols].astype(jnp.float32)
        relay2[:, :, cols] = both.astype(jnp.bfloat16)
        for k in range(1, ngroups):
            to = (group + k) % ngroups
            send(relay2.at[to, :, cols], land2.at[k - 1, :, cols],
                 send2.at[k - 1, c], recv2.at[k - 1, c], (to * 4 + here_p % 4, here_c))
        total[:, :, cols] = both

    def share_sums():
        loglik_ref[...] = logliks[here_c]
        for b in range(2):
            cols = slice(b * block, (b + 1) * block)
            sums[0, 0:1, cols] = jnp.sum(count_sum[b].T, axis=0, keepdims=True)
            sums[0, 1:2, cols] = jnp.sum(sq_sum[b].T, axis=0, keepdims=True)
        for k in range(1, npts):
            send(sums.at[0], sums.at[k], sum_send.at[k - 1], sum_recv.at[k - 1],
                 ((here_p + k) % npts, here_c))

    def column(row):
        mine = lax.broadcasted_iota(jnp.int32, (share, owned), 1) == (
            lax.broadcasted_iota(jnp.int32, (share, owned), 0) + here_p * share
        )
        return jnp.sum(jnp.where(mine, row, 0.0), axis=1, keepdims=True)

    def take_sums():
        for k in range(1, npts):
            arrived(sums.at[k], sum_send.at[k - 1], sum_recv.at[k - 1])
        both = sums[0]
        for k in range(1, npts):
            both = both + sums[k]
        return column(both[0:1]), column(both[1:2])

    lag = 2
    for t in range(pieces + lag + 2):
        if t < pieces:
            make(t)
        if t == 1:
            share_sums()
        if lag <= t < pieces + lag:
            halve(t - lag)
        if lag < t <= pieces + lag:
            spread(t - lag - 1)
        if t == pieces:
            counts, sqsum = take_sums()
            scale = 1.0 / (counts + 1.0)
            var_old = column(var_row[...])
            cross = jnp.zeros((share, 1), jnp.float32)
            norm = jnp.zeros((share, 1), jnp.float32)
        if t >= pieces:
            ready = [t - lag - 2] if t > pieces else list(range(pieces - lag - 1))
            for c in ready:
                cols = pl.ds(c * piece, piece)
                w = total[group, :, cols]
                for k in range(1, ngroups):
                    arrived(land2.at[k - 1, :, cols], send2.at[k - 1, c], recv2.at[k - 1, c])
                    w = w + land2[k - 1, :, cols].astype(jnp.float32)
                new = (w + mu_old[:, cols].astype(jnp.float32)) * scale
                mean_ref[:, cols] = new
                cross = cross + jnp.sum(new * w, axis=1, keepdims=True)
                norm = norm + jnp.sum(new * new, axis=1, keepdims=True)
    resid = sqsum - 2.0 * cross + counts * norm + width * var_old
    new_var = resid / (width * (counts + 1.0))
    new_logw = jnp.log((counts + 1.0) / float(rows * ncomp * npts + owned * ncomp))
    eye_s = lax.broadcasted_iota(jnp.int32, (share, share), 0) == lax.broadcasted_iota(
        jnp.int32, (share, share), 1
    )
    newvar_ref[...] = jnp.sum(jnp.where(eye_s, new_var, 0.0), axis=0, keepdims=True)
    newlogw_ref[...] = jnp.sum(jnp.where(eye_s, new_logw, 0.0), axis=0, keepdims=True)

    for copy in sends:
        copy.wait_send()


def copy_kernel(*refs):
    count = len(refs) // 2
    copies = [
        pltpu.make_async_copy(refs[i], refs[count + i], refs[-1].at[i]) for i in range(count)
    ]
    for copy in copies:
        copy.start()
    for copy in copies:
        copy.wait()


def on_device(ncomp, npts, points, candidates, means, variances, log_weights):
    rows, width = points.shape
    owned = means.shape[0]
    share = owned // npts
    ngroups = npts // 4
    pieces = 8
    ncand = candidates.shape[1]
    ny = ncomp // 2
    aux_rows = -(-(ncand + 1) // 8) * 8
    f32, bf16 = jnp.float32, jnp.bfloat16
    dma = pltpu.SemaphoreType.DMA
    vmem = pl.BlockSpec(memory_space=pltpu.VMEM)
    anywhere = pl.BlockSpec(memory_space=pl.ANY)
    results = pl.pallas_call(
        functools.partial(em_kernel, ncomp, npts, pieces),
        out_shape=(
            jax.ShapeDtypeStruct((1, rows), f32),
            jax.ShapeDtypeStruct((share, width), f32),
            jax.ShapeDtypeStruct((1, share), f32),
            jax.ShapeDtypeStruct((1, share), f32),
        ),
        in_specs=[anywhere] * 6,
        out_specs=(vmem, vmem, vmem, vmem),
        scratch_shapes=[
            pltpu.VMEM((ncomp, rows, width), bf16),
            pltpu.VMEM((owned, width), bf16),
            pltpu.VMEM((share, width), bf16),
            pltpu.VMEM((ncand, rows), jnp.int32),
            pltpu.VMEM((1, owned), f32),
            pltpu.VMEM((1, owned), f32),
            pltpu.VMEM((ncomp, aux_rows, rows), f32),
            pltpu.VMEM((ncomp, owned, rows), f32),
            pltpu.VMEM((ncomp, ncomp, 2, rows), f32),
            pltpu.VMEM((ncomp, 1, rows), f32),
            pltpu.VMEM((owned, ncomp * rows), bf16),
            pltpu.VMEM((npts, 2, owned), f32),
            pltpu.VMEM((2, 2, ngroups, share, width), bf16),
            pltpu.VMEM((2, ngroups, share, width), bf16),
            pltpu.VMEM((ngroups, share, width), f32),
            pltpu.VMEM((ngroups, share, width), bf16),
            pltpu.VMEM((ngroups, share, width), bf16),
            pltpu.VMEM((ngroups, share, width), f32),
            pltpu.VMEM((ngroups, share, width), bf16),
            pltpu.VMEM((ngroups - 1, share, width), bf16),
            dma((6,)),
            dma((ny - 1, pieces)), dma((ny - 1, pieces)),
            dma((1,)), dma((1,)),
            dma((ny - 1, pieces)), dma((ny - 1, pieces)),
            dma((ncomp - 1,)), dma((ncomp - 1,)),
            dma((ncomp - 1, ncomp)), dma((ncomp - 1, ncomp)),
            dma((npts - 1,)), dma((npts - 1,)),
            dma((pieces,)), dma((pieces,)),
            dma((pieces,)), dma((pieces,)),
            dma((ngroups - 1, pieces)), dma((ngroups - 1, pieces)),
        ],
        compiler_params=pltpu.CompilerParams(
            collective_id=0, has_side_effects=True, vmem_limit_bytes=60 * 1024 * 1024
        ),
        name="em_step",
    )(
        points, candidates.T, means, means.reshape(npts, share, width),
        variances.reshape(1, owned), log_weights.reshape(1, owned),
    )
    loglik, new_means, new_var, new_logw = pl.pallas_call(
        copy_kernel,
        out_shape=tuple(jax.ShapeDtypeStruct(x.shape, x.dtype) for x in results),
        in_specs=[anywhere] * len(results),
        out_specs=(anywhere,) * len(results),
        scratch_shapes=[dma((len(results),))],
        compiler_params=pltpu.CompilerParams(vmem_limit_bytes=60 * 1024 * 1024),
        name="write_results",
    )(*results)
    return (
        loglik.reshape(rows),
        new_means.reshape(1, share, width),
        new_var,
        new_logw,
    )


def solution(mesh):
    return jax.shard_map(
        functools.partial(on_device, mesh.shape["comp"], mesh.shape["pts"]),
        mesh=mesh,
        in_specs=(
            P(("pts", "comp"), None),
            P(("pts", "comp"), None),
            P("comp", None),
            P("comp"),
            P("comp"),
        ),
        out_specs=(P(("pts", "comp")), P("comp", "pts", None), P("comp", "pts"), P("comp", "pts")),
        check_vma=False,
    )
```

```python
import functools
import math

import jax
import jax.numpy as jnp
from jax import lax
from jax.experimental import pallas as pl
from jax.experimental.pallas import tpu as pltpu
from jax.sharding import PartitionSpec as P

MESH = pl.DeviceIdType.MESH
LANES = 128
LOW = -3.0e38


def em_kernel(
    ncomp, npts, pieces,
    points_ref, cand_ref, means_ref, var_ref, logw_ref,
    loglik_ref, wsum_ref, sums_ref,
    gathered, means, cands, var_row, logw_row, aux, logp, stats, logliks, resp16, sums,
    wsend, land0, kept, relay1, land1, total, relay2, land2,
    load_sem, y_send, y_recv, sib_send, sib_recv, fwd_send, fwd_recv,
    aux_send, aux_recv, st_send, st_recv, sum_send, sum_recv,
    send0, recv0, send1, recv1, send2, recv2,
):
    here_c, here_p = lax.axis_index("comp"), lax.axis_index("pts")
    ny, ngroups = ncomp // 2, npts // 4
    rows, width = points_ref.shape
    owned = means_ref.shape[0]
    block = owned // 2
    share = owned // npts
    piece = width // pieces
    ncand = cand_ref.shape[0]
    y, core = here_c // 2, here_c % 2
    other_core = 1 - core
    sibling = y * 2 + other_core
    group = here_p // 4
    bits = (here_p % 2, (here_p // 2) % 2)
    partners = (here_p + 1 - 2 * bits[0], here_p + 2 - 4 * bits[1])

    def order(c):
        return (1, 0) if c % 4 == 1 else (0, 1)

    barrier = pltpu.get_barrier_semaphore()
    for k in range(1, ncomp):
        pl.semaphore_signal(
            barrier, inc=1, device_id=(here_p, (here_c + k) % ncomp), device_id_type=MESH
        )
    for k in range(1, npts):
        pl.semaphore_signal(
            barrier, inc=1, device_id=((here_p + k) % npts, here_c), device_id_type=MESH
        )

    loads = [
        pltpu.make_async_copy(src, dst, load_sem.at[i])
        for i, (src, dst) in enumerate(
            [(cand_ref, cands)]
            + [
                (points_ref.at[:, pl.ds(c * piece, piece)], gathered.at[here_c, c])
                for c in range(pieces)
            ]
            + [(means_ref, means), (var_ref, var_row), (logw_ref, logw_row)]
        )
    ]
    for load in loads:
        load.start()

    for load in loads[: pieces + 1]:
        load.wait()

    def add_point_squares(c, acc):
        for j in range(piece // LANES):
            x = gathered[here_c, c, :, j * LANES : (j + 1) * LANES].astype(jnp.float32)
            acc = acc + x * x
        return acc

    sq = lax.fori_loop(0, pieces, add_point_squares, jnp.zeros((rows, LANES), jnp.float32))
    xx_row = jnp.sum(sq.T, axis=0, keepdims=True)
    aux[here_c] = jnp.concatenate(
        [cands[...].astype(jnp.float32), xx_row]
        + [jnp.zeros((aux.shape[1] - ncand - 1, rows), jnp.float32)],
        axis=0,
    )
    pl.semaphore_wait(barrier, ncomp + npts - 2)

    sends = []

    def send(src, dst, s_sem, r_sem, device):
        copy = pltpu.make_async_remote_copy(
            src_ref=src, dst_ref=dst, send_sem=s_sem, recv_sem=r_sem,
            device_id=device, device_id_type=MESH,
        )
        copy.start()
        sends.append(copy)

    def arrived(dst, s_sem, r_sem):
        pltpu.make_async_remote_copy(
            src_ref=dst, dst_ref=dst, send_sem=s_sem, recv_sem=r_sem,
            device_id=(here_p, sibling), device_id_type=MESH,
        ).wait_recv()

    def part(slot, c):
        return gathered.at[slot, c]

    for c in range(pieces):
        for k in range(1, ny):
            send(part(here_c, c), part(here_c, c), y_send.at[k - 1, c], y_recv.at[k - 1, c],
                 (here_p, ((y + k) % ny) * 2 + core))
        if c == 0:
            for k in range(1, ncomp):
                send(aux.at[here_c], aux.at[here_c], aux_send.at[k - 1], aux_recv.at[k - 1],
                     (here_p, (here_c + k) % ncomp))
    send(gathered.at[here_c], gathered.at[here_c], sib_send.at[0], sib_recv.at[0],
         (here_p, sibling))

    for load in loads[pieces + 1 :]:
        load.wait()

    def dot_t(slot, c):
        return lax.dot_general(
            means[:, pl.ds(c * piece, piece)], gathered[slot, c],
            (((1,), (1,)), ((), ())), preferred_element_type=jnp.float32,
        )

    def dot_all(slot):
        g = dot_t(slot, 0)
        for c in range(1, pieces):
            g = g + dot_t(slot, c)
        return g

    def add_mean_squares(j, acc):
        x = means[:, pl.ds(pl.multiple_of(j * LANES, LANES), LANES)].astype(jnp.float32)
        return acc + x * x

    sq = lax.fori_loop(
        0, width // LANES, add_mean_squares, jnp.zeros((owned, LANES), jnp.float32)
    )
    mm = jnp.sum(sq, axis=1, keepdims=True)
    eye_k = lax.broadcasted_iota(jnp.int32, (owned, owned), 0) == lax.broadcasted_iota(
        jnp.int32, (owned, owned), 1
    )
    var = jnp.sum(jnp.where(eye_k, var_row[...], 0.0), axis=1, keepdims=True)
    logw = jnp.sum(jnp.where(eye_k, logw_row[...], 0.0), axis=1, keepdims=True)
    const = logw - 0.5 * width * jnp.log(2.0 * math.pi * var)
    two_var = 2.0 * var

    def named(s, b):
        number = (here_c * 2 + b).astype(jnp.float32)
        hit = aux[s, 0:1, :] == number
        for j in range(1, ncand):
            hit = hit | (aux[s, j : j + 1, :] == number)
        return hit

    def finish(s, g):
        xx = aux[s, ncand : ncand + 1, :]
        lp = const - (xx - 2.0 * g + mm) / two_var
        logp[s] = lp
        tops, totals = [], []
        for b in range(2):
            half = lp[b * block : (b + 1) * block]
            top = jnp.max(half, axis=0, keepdims=True)
            hit = named(s, b)
            part_sum = jnp.sum(jnp.exp(half - top), axis=0, keepdims=True)
            tops.append(jnp.where(hit, top, LOW))
            totals.append(jnp.where(hit, part_sum, 0.0))
        top = jnp.maximum(tops[0], tops[1])
        stats[here_c, s, 0:1, :] = top
        stats[here_c, s, 1:2, :] = totals[0] * jnp.exp(tops[0] - top) + totals[1] * jnp.exp(
            tops[1] - top
        )
        for k in range(1, ncomp):
            send(stats.at[here_c, s], stats.at[here_c, s], st_send.at[k - 1, s],
                 st_recv.at[k - 1, s], (here_p, (here_c + k) % ncomp))

    finish(here_c, dot_all(here_c))
    for k in range(1, ncomp):
        arrived(aux.at[(here_c + ncomp - k) % ncomp], aux_send.at[k - 1], aux_recv.at[k - 1])
    arrived(gathered.at[sibling], sib_send.at[0], sib_recv.at[0])
    finish(sibling, dot_all(sibling))

    def accumulate(slot, c):
        g = dot_t(slot, c)
        if c:
            g = logp[slot] + g
        if c < pieces - 1:
            logp[slot] = g
        else:
            finish(slot, g)

    def take_forwarded(c):
        for k in range(1, ny):
            slot = ((y + ny - k) % ny) * 2 + other_core
            arrived(part(slot, c), fwd_send.at[k - 1, c], fwd_recv.at[k - 1, c])
            accumulate(slot, c)

    for c in range(pieces):
        for k in range(1, ny):
            slot = ((y + ny - k) % ny) * 2 + core
            arrived(part(slot, c), y_send.at[k - 1, c], y_recv.at[k - 1, c])
            send(part(slot, c), part(slot, c), fwd_send.at[k - 1, c], fwd_recv.at[k - 1, c],
                 (here_p, sibling))
            accumulate(slot, c)
        if c:
            take_forwarded(c - 1)
    take_forwarded(pieces - 1)

    for k in range(1, ncomp):
        owner = (here_c + ncomp - k) % ncomp
        for s in range(ncomp):
            arrived(stats.at[owner, s], st_send.at[k - 1, s], st_recv.at[k - 1, s])

    count_sum = [jnp.zeros((block, rows), jnp.float32) for _ in range(2)]
    sq_sum = [jnp.zeros((block, rows), jnp.float32) for _ in range(2)]
    for s in range(ncomp):
        lanes = slice(s * rows, (s + 1) * rows)
        tops = [stats[o, s, 0:1, :] for o in range(ncomp)]
        top = functools.reduce(jnp.maximum, tops)
        weight = stats[0, s, 1:2, :] * jnp.exp(tops[0] - top)
        for o in range(1, ncomp):
            weight = weight + stats[o, s, 1:2, :] * jnp.exp(tops[o] - top)
        loglik = top + jnp.log(weight)
        logliks[s] = loglik
        xx = aux[s, ncand : ncand + 1, :]
        for b in range(2):
            resp = jnp.where(
                named(s, b), jnp.exp(logp[s, b * block : (b + 1) * block, :] - loglik), 0.0
            )
            resp16[b * block : (b + 1) * block, lanes] = resp.astype(jnp.bfloat16)
            count_sum[b] = count_sum[b] + resp
            sq_sum[b] = sq_sum[b] + resp * xx

    def make(c):
        data = gathered[:, c].reshape(ncomp * rows, piece)
        w = jnp.dot(resp16[...], data, preferred_element_type=jnp.float32)
        first, second = order(c)
        for g in range(ngroups):
            for n in range(4):
                dest = (n % 2, n // 2)
                start = (g * 4 + n) * share
                wsend[c, dest[first], dest[second], g] = w[start : start + share].astype(
                    jnp.bfloat16
                )
        send(wsend.at[c, 1 - bits[first]], land0.at[c], send0.at[c], recv0.at[c],
             (partners[first], here_c))

    def halve(c):
        first, second = order(c)
        mine, other = bits[second], 1 - bits[second]
        arrived(land0.at[c], send0.at[c], recv0.at[c])
        relay1[c] = (
            wsend[c, bits[first], other].astype(jnp.float32) + land0[c, other].astype(jnp.float32)
        ).astype(jnp.bfloat16)
        send(relay1.at[c], land1.at[c], send1.at[c], recv1.at[c], (partners[second], here_c))
        kept[c] = wsend[c, bits[first], mine].astype(jnp.float32) + land0[c, mine].astype(
            jnp.float32
        )

    def spread(c):
        arrived(land1.at[c], send1.at[c], recv1.at[c])
        both = kept[c] + land1[c].astype(jnp.float32)
        relay2[c] = both.astype(jnp.bfloat16)
        for k in range(1, ngroups):
            to = (group + k) % ngroups
            send(relay2.at[c, to], land2.at[k - 1, c], send2.at[k - 1, c], recv2.at[k - 1, c],
                 (to * 4 + here_p % 4, here_c))
        total[c] = both

    def share_sums():
        loglik_ref[...] = logliks[here_c]
        for b in range(2):
            cols = slice(b * block, (b + 1) * block)
            sums[0, 0:1, cols] = jnp.sum(count_sum[b].T, axis=0, keepdims=True)
            sums[0, 1:2, cols] = jnp.sum(sq_sum[b].T, axis=0, keepdims=True)
        for k in range(1, npts):
            send(sums.at[0], sums.at[k], sum_send.at[k - 1], sum_recv.at[k - 1],
                 ((here_p + k) % npts, here_c))

    def take_sums():
        for k in range(1, npts):
            arrived(sums.at[k], sum_send.at[k - 1], sum_recv.at[k - 1])
        both = sums[0]
        for k in range(1, npts):
            both = both + sums[k]
        sums_ref[...] = both

    lag = 2
    for t in range(pieces + lag + 2):
        if t < pieces:
            make(t)
        if t == 1:
            share_sums()
        if lag <= t < pieces + lag:
            halve(t - lag)
        if lag < t <= pieces + lag:
            spread(t - lag - 1)
        if t == pieces:
            take_sums()
        if t >= pieces:
            ready = [t - lag - 2] if t > pieces else list(range(pieces - lag - 1))
            for c in ready:
                w = total[c, group]
                for k in range(1, ngroups):
                    arrived(land2.at[k - 1, c], send2.at[k - 1, c], recv2.at[k - 1, c])
                    w = w + land2[k - 1, c].astype(jnp.float32)
                wsum_ref[:, c * piece : (c + 1) * piece] = w

    for copy in sends:
        copy.wait_send()


def update_kernel(
    npoints, ncomponents,
    loglik_ref, wsum_ref, sums_ref, shares_ref, var_ref,
    loglik_out, mean_ref, newvar_ref, newlogw_ref,
    mu_old, load_sem,
):
    here_p = lax.axis_index("pts")
    load = pltpu.make_async_copy(shares_ref.at[here_p], mu_old, load_sem)
    load.start()
    share, width = wsum_ref.shape
    owned = sums_ref.shape[1]
    mine = lax.broadcasted_iota(jnp.int32, (share, owned), 1) == (
        lax.broadcasted_iota(jnp.int32, (share, owned), 0) + here_p * share
    )

    def column(row):
        return jnp.sum(jnp.where(mine, row, 0.0), axis=1, keepdims=True)

    loglik_out[...] = loglik_ref[...]
    counts, sqsum = column(sums_ref[0:1, :]), column(sums_ref[1:2, :])
    var_old = column(var_ref[...])
    scale = 1.0 / (counts + 1.0)
    cross = jnp.zeros((share, LANES), jnp.float32)
    norm = jnp.zeros((share, LANES), jnp.float32)
    load.wait()
    for j in range(width // LANES):
        cols = slice(j * LANES, (j + 1) * LANES)
        w = wsum_ref[:, cols]
        new = (w + mu_old[:, cols].astype(jnp.float32)) * scale
        mean_ref[:, cols] = new
        cross = cross + new * w
        norm = norm + new * new
    cross = jnp.sum(cross, axis=1, keepdims=True)
    norm = jnp.sum(norm, axis=1, keepdims=True)
    resid = sqsum - 2.0 * cross + counts * norm + width * var_old
    new_var = resid / (width * (counts + 1.0))
    new_logw = jnp.log((counts + 1.0) / float(npoints + ncomponents))
    eye = lax.broadcasted_iota(jnp.int32, (share, share), 0) == lax.broadcasted_iota(
        jnp.int32, (share, share), 1
    )
    newvar_ref[...] = jnp.sum(jnp.where(eye, new_var, 0.0), axis=0, keepdims=True)
    newlogw_ref[...] = jnp.sum(jnp.where(eye, new_logw, 0.0), axis=0, keepdims=True)


def on_device(ncomp, npts, points, candidates, means, variances, log_weights):
    rows, width = points.shape
    owned = means.shape[0]
    share = owned // npts
    ngroups = npts // 4
    pieces = 8
    ncand = candidates.shape[1]
    ny = ncomp // 2
    aux_rows = -(-(ncand + 1) // 8) * 8
    f32, bf16 = jnp.float32, jnp.bfloat16
    dma = pltpu.SemaphoreType.DMA
    vmem = pl.BlockSpec(memory_space=pltpu.VMEM)
    anywhere = pl.BlockSpec(memory_space=pl.ANY)
    piece = width // pieces
    loglik, wsum, sums = pl.pallas_call(
        functools.partial(em_kernel, ncomp, npts, pieces),
        out_shape=(
            jax.ShapeDtypeStruct((1, rows), f32),
            jax.ShapeDtypeStruct((share, width), f32),
            jax.ShapeDtypeStruct((2, owned), f32),
        ),
        in_specs=[anywhere] * 5,
        out_specs=(vmem, vmem, vmem),
        scratch_shapes=[
            pltpu.VMEM((ncomp, pieces, rows, piece), bf16),
            pltpu.VMEM((owned, width), bf16),
            pltpu.VMEM((ncand, rows), jnp.int32),
            pltpu.VMEM((1, owned), f32),
            pltpu.VMEM((1, owned), f32),
            pltpu.VMEM((ncomp, aux_rows, rows), f32),
            pltpu.VMEM((ncomp, owned, rows), f32),
            pltpu.VMEM((ncomp, ncomp, 2, rows), f32),
            pltpu.VMEM((ncomp, 1, rows), f32),
            pltpu.VMEM((owned, ncomp * rows), bf16),
            pltpu.VMEM((npts, 2, owned), f32),
            pltpu.VMEM((pieces, 2, 2, ngroups, share, piece), bf16),
            pltpu.VMEM((pieces, 2, ngroups, share, piece), bf16),
            pltpu.VMEM((pieces, ngroups, share, piece), f32),
            pltpu.VMEM((pieces, ngroups, share, piece), bf16),
            pltpu.VMEM((pieces, ngroups, share, piece), bf16),
            pltpu.VMEM((pieces, ngroups, share, piece), f32),
            pltpu.VMEM((pieces, ngroups, share, piece), bf16),
            pltpu.VMEM((ngroups - 1, pieces, share, piece), bf16),
            dma((pieces + 4,)),
            dma((ny - 1, pieces)), dma((ny - 1, pieces)),
            dma((1,)), dma((1,)),
            dma((ny - 1, pieces)), dma((ny - 1, pieces)),
            dma((ncomp - 1,)), dma((ncomp - 1,)),
            dma((ncomp - 1, ncomp)), dma((ncomp - 1, ncomp)),
            dma((npts - 1,)), dma((npts - 1,)),
            dma((pieces,)), dma((pieces,)),
            dma((pieces,)), dma((pieces,)),
            dma((ngroups - 1, pieces)), dma((ngroups - 1, pieces)),
        ],
        compiler_params=pltpu.CompilerParams(
            collective_id=0, has_side_effects=True, vmem_limit_bytes=60 * 1024 * 1024
        ),
        name="em_step",
    )(
        points, candidates.T, means, variances.reshape(1, owned), log_weights.reshape(1, owned)
    )
    loglik, new_means, new_var, new_logw = pl.pallas_call(
        functools.partial(update_kernel, rows * ncomp * npts, owned * ncomp),
        out_shape=(
            jax.ShapeDtypeStruct((1, rows), f32),
            jax.ShapeDtypeStruct((share, width), f32),
            jax.ShapeDtypeStruct((1, share), f32),
            jax.ShapeDtypeStruct((1, share), f32),
        ),
        in_specs=[vmem, vmem, vmem, anywhere, vmem],
        out_specs=(vmem, vmem, vmem, vmem),
        scratch_shapes=[pltpu.VMEM((share, width), bf16), dma],
        compiler_params=pltpu.CompilerParams(vmem_limit_bytes=60 * 1024 * 1024),
        name="update",
    )(loglik, wsum, sums, means.reshape(npts, share, width), variances.reshape(1, owned))
    return (
        loglik.reshape(rows),
        new_means.reshape(1, share, width),
        new_var,
        new_logw,
    )


def solution(mesh):
    return jax.shard_map(
        functools.partial(on_device, mesh.shape["comp"], mesh.shape["pts"]),
        mesh=mesh,
        in_specs=(
            P(("pts", "comp"), None),
            P(("pts", "comp"), None),
            P("comp", None),
            P("comp"),
            P("comp"),
        ),
        out_specs=(P(("pts", "comp")), P("comp", "pts", None), P("comp", "pts"), P("comp", "pts")),
        check_vma=False,
    )
```

```python
import functools
import math

import jax
import jax.numpy as jnp
from jax import lax
from jax.experimental import pallas as pl
from jax.experimental.pallas import tpu as pltpu
from jax.sharding import PartitionSpec as P

MESH = pl.DeviceIdType.MESH
LANES = 128
LOW = -3.0e38


def em_kernel(
    ncomp, npts, pieces,
    points_ref, cand_ref, means_ref, var_ref, logw_ref,
    loglik_ref, wsum_ref, sums_ref,
    gathered, means, cands, var_row, logw_row, aux, logp, stats, logliks, resp16, sums,
    wsend, land0, kept, relay1, land1, total, relay2, land2,
    load_sem, y_send, y_recv, sib_send, sib_recv, fwd_send, fwd_recv,
    aux_send, aux_recv, st_send, st_recv, sum_send, sum_recv,
    send0, recv0, send1, recv1, send2, recv2,
):
    here_c, here_p = lax.axis_index("comp"), lax.axis_index("pts")
    ny, ngroups = ncomp // 2, npts // 4
    rows, width = points_ref.shape
    owned = means_ref.shape[0]
    block = owned // 2
    share = owned // npts
    piece = width // pieces
    ncand = cand_ref.shape[0]
    y, core = here_c // 2, here_c % 2
    other_core = 1 - core
    sibling = y * 2 + other_core
    group = here_p // 4
    bits = (here_p % 2, (here_p // 2) % 2)
    partners = (here_p + 1 - 2 * bits[0], here_p + 2 - 4 * bits[1])

    def order(c):
        return (1, 0) if c % 4 == 1 else (0, 1)

    barrier = pltpu.get_barrier_semaphore()
    for k in range(1, ncomp):
        pl.semaphore_signal(
            barrier, inc=1, device_id=(here_p, (here_c + k) % ncomp), device_id_type=MESH
        )
    for k in range(1, npts):
        pl.semaphore_signal(
            barrier, inc=1, device_id=((here_p + k) % npts, here_c), device_id_type=MESH
        )

    loads = [
        pltpu.make_async_copy(src, dst, load_sem.at[i])
        for i, (src, dst) in enumerate(
            [(cand_ref, cands)]
            + [
                (points_ref.at[:, pl.ds(c * piece, piece)], gathered.at[here_c, c])
                for c in range(pieces)
            ]
            + [(means_ref, means), (var_ref, var_row), (logw_ref, logw_row)]
        )
    ]
    for load in loads:
        load.start()

    for load in loads[: pieces + 1]:
        load.wait()

    def add_point_squares(c, acc):
        for j in range(piece // LANES):
            x = gathered[here_c, c, :, j * LANES : (j + 1) * LANES].astype(jnp.float32)
            acc = acc + x * x
        return acc

    sq = lax.fori_loop(0, pieces, add_point_squares, jnp.zeros((rows, LANES), jnp.float32))
    xx_row = jnp.sum(sq.T, axis=0, keepdims=True)
    aux[here_c] = jnp.concatenate(
        [cands[...].astype(jnp.float32), xx_row]
        + [jnp.zeros((aux.shape[1] - ncand - 1, rows), jnp.float32)],
        axis=0,
    )
    pl.semaphore_wait(barrier, ncomp + npts - 2)

    sends = []

    def send(src, dst, s_sem, r_sem, device):
        copy = pltpu.make_async_remote_copy(
            src_ref=src, dst_ref=dst, send_sem=s_sem, recv_sem=r_sem,
            device_id=device, device_id_type=MESH,
        )
        copy.start()
        sends.append(copy)

    def arrived(dst, s_sem, r_sem):
        pltpu.make_async_remote_copy(
            src_ref=dst, dst_ref=dst, send_sem=s_sem, recv_sem=r_sem,
            device_id=(here_p, sibling), device_id_type=MESH,
        ).wait_recv()

    def part(slot, c):
        return gathered.at[slot, c]

    for c in range(pieces):
        for k in range(1, ny):
            send(part(here_c, c), part(here_c, c), y_send.at[k - 1, c], y_recv.at[k - 1, c],
                 (here_p, ((y + k) % ny) * 2 + core))
        if c == 0:
            for k in range(1, ncomp):
                send(aux.at[here_c], aux.at[here_c], aux_send.at[k - 1], aux_recv.at[k - 1],
                     (here_p, (here_c + k) % ncomp))
    send(gathered.at[here_c], gathered.at[here_c], sib_send.at[0], sib_recv.at[0],
         (here_p, sibling))

    for load in loads[pieces + 1 :]:
        load.wait()

    def dot_t(slot, c):
        return lax.dot_general(
            means[:, pl.ds(c * piece, piece)], gathered[slot, c],
            (((1,), (1,)), ((), ())), preferred_element_type=jnp.float32,
        )

    def dot_all(slot):
        g = dot_t(slot, 0)
        for c in range(1, pieces):
            g = g + dot_t(slot, c)
        return g

    def add_mean_squares(j, acc):
        x = means[:, pl.ds(pl.multiple_of(j * LANES, LANES), LANES)].astype(jnp.float32)
        return acc + x * x

    sq = lax.fori_loop(
        0, width // LANES, add_mean_squares, jnp.zeros((owned, LANES), jnp.float32)
    )
    mm = jnp.sum(sq, axis=1, keepdims=True)
    eye_k = lax.broadcasted_iota(jnp.int32, (owned, owned), 0) == lax.broadcasted_iota(
        jnp.int32, (owned, owned), 1
    )
    var = jnp.sum(jnp.where(eye_k, var_row[...], 0.0), axis=1, keepdims=True)
    logw = jnp.sum(jnp.where(eye_k, logw_row[...], 0.0), axis=1, keepdims=True)
    const = logw - 0.5 * width * jnp.log(2.0 * math.pi * var)
    two_var = 2.0 * var

    def named(s, b):
        number = (here_c * 2 + b).astype(jnp.float32)
        hit = aux[s, 0:1, :] == number
        for j in range(1, ncand):
            hit = hit | (aux[s, j : j + 1, :] == number)
        return hit

    def finish(s, g):
        xx = aux[s, ncand : ncand + 1, :]
        lp = const - (xx - 2.0 * g + mm) / two_var
        logp[s] = lp
        tops, totals = [], []
        for b in range(2):
            half = lp[b * block : (b + 1) * block]
            top = jnp.max(half, axis=0, keepdims=True)
            hit = named(s, b)
            part_sum = jnp.sum(jnp.exp(half - top), axis=0, keepdims=True)
            tops.append(jnp.where(hit, top, LOW))
            totals.append(jnp.where(hit, part_sum, 0.0))
        top = jnp.maximum(tops[0], tops[1])
        stats[here_c, s, 0:1, :] = top
        stats[here_c, s, 1:2, :] = totals[0] * jnp.exp(tops[0] - top) + totals[1] * jnp.exp(
            tops[1] - top
        )
        for k in range(1, ncomp):
            send(stats.at[here_c, s], stats.at[here_c, s], st_send.at[k - 1, s],
                 st_recv.at[k - 1, s], (here_p, (here_c + k) % ncomp))

    finish(here_c, dot_all(here_c))
    for k in range(1, ncomp):
        arrived(aux.at[(here_c + ncomp - k) % ncomp], aux_send.at[k - 1], aux_recv.at[k - 1])
    arrived(gathered.at[sibling], sib_send.at[0], sib_recv.at[0])
    finish(sibling, dot_all(sibling))

    def accumulate(slot, c):
        g = dot_t(slot, c)
        if c:
            g = logp[slot] + g
        if c < pieces - 1:
            logp[slot] = g
        else:
            finish(slot, g)

    def take_forwarded(c):
        for k in range(1, ny):
            slot = ((y + ny - k) % ny) * 2 + other_core
            arrived(part(slot, c), fwd_send.at[k - 1, c], fwd_recv.at[k - 1, c])
            accumulate(slot, c)

    for c in range(pieces):
        for k in range(1, ny):
            slot = ((y + ny - k) % ny) * 2 + core
            arrived(part(slot, c), y_send.at[k - 1, c], y_recv.at[k - 1, c])
            send(part(slot, c), part(slot, c), fwd_send.at[k - 1, c], fwd_recv.at[k - 1, c],
                 (here_p, sibling))
            accumulate(slot, c)
        if c:
            take_forwarded(c - 1)
    take_forwarded(pieces - 1)

    for k in range(1, ncomp):
        owner = (here_c + ncomp - k) % ncomp
        for s in range(ncomp):
            arrived(stats.at[owner, s], st_send.at[k - 1, s], st_recv.at[k - 1, s])

    count_sum = [jnp.zeros((block, rows), jnp.float32) for _ in range(2)]
    sq_sum = [jnp.zeros((block, rows), jnp.float32) for _ in range(2)]
    for s in range(ncomp):
        lanes = slice(s * rows, (s + 1) * rows)
        tops = [stats[o, s, 0:1, :] for o in range(ncomp)]
        top = functools.reduce(jnp.maximum, tops)
        weight = stats[0, s, 1:2, :] * jnp.exp(tops[0] - top)
        for o in range(1, ncomp):
            weight = weight + stats[o, s, 1:2, :] * jnp.exp(tops[o] - top)
        loglik = top + jnp.log(weight)
        logliks[s] = loglik
        xx = aux[s, ncand : ncand + 1, :]
        for b in range(2):
            resp = jnp.where(
                named(s, b), jnp.exp(logp[s, b * block : (b + 1) * block, :] - loglik), 0.0
            )
            resp16[b * block : (b + 1) * block, lanes] = resp.astype(jnp.bfloat16)
            count_sum[b] = count_sum[b] + resp
            sq_sum[b] = sq_sum[b] + resp * xx

    def make(c):
        data = gathered[:, c].reshape(ncomp * rows, piece)
        w = jnp.dot(resp16[...], data, preferred_element_type=jnp.float32)
        first, second = order(c)
        for g in range(ngroups):
            for n in range(4):
                dest = (n % 2, n // 2)
                start = (g * 4 + n) * share
                wsend[c, dest[first], dest[second], g] = w[start : start + share].astype(
                    jnp.bfloat16
                )
        send(wsend.at[c, 1 - bits[first]], land0.at[c], send0.at[c], recv0.at[c],
             (partners[first], here_c))

    def halve(c):
        first, second = order(c)
        mine, other = bits[second], 1 - bits[second]
        arrived(land0.at[c], send0.at[c], recv0.at[c])
        relay1[c] = (
            wsend[c, bits[first], other].astype(jnp.float32) + land0[c, other].astype(jnp.float32)
        ).astype(jnp.bfloat16)
        send(relay1.at[c], land1.at[c], send1.at[c], recv1.at[c], (partners[second], here_c))
        kept[c] = wsend[c, bits[first], mine].astype(jnp.float32) + land0[c, mine].astype(
            jnp.float32
        )

    def spread(c):
        arrived(land1.at[c], send1.at[c], recv1.at[c])
        both = kept[c] + land1[c].astype(jnp.float32)
        relay2[c] = both.astype(jnp.bfloat16)
        for k in range(1, ngroups):
            to = (group + k) % ngroups
            send(relay2.at[c, to], land2.at[k - 1, c], send2.at[k - 1, c], recv2.at[k - 1, c],
                 (to * 4 + here_p % 4, here_c))
        total[c] = both

    def share_sums():
        loglik_ref[...] = logliks[here_c]
        for b in range(2):
            cols = slice(b * block, (b + 1) * block)
            sums[0, 0:1, cols] = jnp.sum(count_sum[b].T, axis=0, keepdims=True)
            sums[0, 1:2, cols] = jnp.sum(sq_sum[b].T, axis=0, keepdims=True)
        for k in range(1, npts):
            send(sums.at[0], sums.at[k], sum_send.at[k - 1], sum_recv.at[k - 1],
                 ((here_p + k) % npts, here_c))

    def take_sums():
        for k in range(1, npts):
            arrived(sums.at[k], sum_send.at[k - 1], sum_recv.at[k - 1])
        both = sums[0]
        for k in range(1, npts):
            both = both + sums[k]
        sums_ref[...] = both

    for c in range(pieces):
        make(c)
    share_sums()
    for t in range(pieces + 2):
        if t < pieces:
            halve(t)
        if 1 <= t <= pieces:
            spread(t - 1)
        if t == 2:
            take_sums()
        if t >= 2:
            c = t - 2
            w = total[c, group]
            for k in range(1, ngroups):
                arrived(land2.at[k - 1, c], send2.at[k - 1, c], recv2.at[k - 1, c])
                w = w + land2[k - 1, c].astype(jnp.float32)
            wsum_ref[:, c * piece : (c + 1) * piece] = w

    for copy in sends:
        copy.wait_send()


def update_kernel(
    npoints, ncomponents,
    loglik_ref, wsum_ref, sums_ref, shares_ref, var_ref,
    loglik_out, mean_ref, newvar_ref, newlogw_ref,
    mu_old, load_sem,
):
    here_p = lax.axis_index("pts")
    load = pltpu.make_async_copy(shares_ref.at[here_p], mu_old, load_sem)
    load.start()
    share, width = wsum_ref.shape
    owned = sums_ref.shape[1]
    mine = lax.broadcasted_iota(jnp.int32, (share, owned), 1) == (
        lax.broadcasted_iota(jnp.int32, (share, owned), 0) + here_p * share
    )

    def column(row):
        return jnp.sum(jnp.where(mine, row, 0.0), axis=1, keepdims=True)

    loglik_out[...] = loglik_ref[...]
    counts, sqsum = column(sums_ref[0:1, :]), column(sums_ref[1:2, :])
    var_old = column(var_ref[...])
    scale = 1.0 / (counts + 1.0)
    cross = jnp.zeros((share, LANES), jnp.float32)
    norm = jnp.zeros((share, LANES), jnp.float32)
    load.wait()
    for j in range(width // LANES):
        cols = slice(j * LANES, (j + 1) * LANES)
        w = wsum_ref[:, cols]
        new = (w + mu_old[:, cols].astype(jnp.float32)) * scale
        mean_ref[:, cols] = new
        cross = cross + new * w
        norm = norm + new * new
    cross = jnp.sum(cross, axis=1, keepdims=True)
    norm = jnp.sum(norm, axis=1, keepdims=True)
    resid = sqsum - 2.0 * cross + counts * norm + width * var_old
    new_var = resid / (width * (counts + 1.0))
    new_logw = jnp.log((counts + 1.0) / float(npoints + ncomponents))
    eye = lax.broadcasted_iota(jnp.int32, (share, share), 0) == lax.broadcasted_iota(
        jnp.int32, (share, share), 1
    )
    newvar_ref[...] = jnp.sum(jnp.where(eye, new_var, 0.0), axis=0, keepdims=True)
    newlogw_ref[...] = jnp.sum(jnp.where(eye, new_logw, 0.0), axis=0, keepdims=True)


def on_device(ncomp, npts, points, candidates, means, variances, log_weights):
    rows, width = points.shape
    owned = means.shape[0]
    share = owned // npts
    ngroups = npts // 4
    pieces = 8
    ncand = candidates.shape[1]
    ny = ncomp // 2
    aux_rows = -(-(ncand + 1) // 8) * 8
    f32, bf16 = jnp.float32, jnp.bfloat16
    dma = pltpu.SemaphoreType.DMA
    vmem = pl.BlockSpec(memory_space=pltpu.VMEM)
    anywhere = pl.BlockSpec(memory_space=pl.ANY)
    piece = width // pieces
    loglik, wsum, sums = pl.pallas_call(
        functools.partial(em_kernel, ncomp, npts, pieces),
        out_shape=(
            jax.ShapeDtypeStruct((1, rows), f32),
            jax.ShapeDtypeStruct((share, width), f32),
            jax.ShapeDtypeStruct((2, owned), f32),
        ),
        in_specs=[anywhere] * 5,
        out_specs=(vmem, vmem, vmem),
        scratch_shapes=[
            pltpu.VMEM((ncomp, pieces, rows, piece), bf16),
            pltpu.VMEM((owned, width), bf16),
            pltpu.VMEM((ncand, rows), jnp.int32),
            pltpu.VMEM((1, owned), f32),
            pltpu.VMEM((1, owned), f32),
            pltpu.VMEM((ncomp, aux_rows, rows), f32),
            pltpu.VMEM((ncomp, owned, rows), f32),
            pltpu.VMEM((ncomp, ncomp, 2, rows), f32),
            pltpu.VMEM((ncomp, 1, rows), f32),
            pltpu.VMEM((owned, ncomp * rows), bf16),
            pltpu.VMEM((npts, 2, owned), f32),
            pltpu.VMEM((pieces, 2, 2, ngroups, share, piece), bf16),
            pltpu.VMEM((pieces, 2, ngroups, share, piece), bf16),
            pltpu.VMEM((pieces, ngroups, share, piece), f32),
            pltpu.VMEM((pieces, ngroups, share, piece), bf16),
            pltpu.VMEM((pieces, ngroups, share, piece), bf16),
            pltpu.VMEM((pieces, ngroups, share, piece), f32),
            pltpu.VMEM((pieces, ngroups, share, piece), bf16),
            pltpu.VMEM((ngroups - 1, pieces, share, piece), bf16),
            dma((pieces + 4,)),
            dma((ny - 1, pieces)), dma((ny - 1, pieces)),
            dma((1,)), dma((1,)),
            dma((ny - 1, pieces)), dma((ny - 1, pieces)),
            dma((ncomp - 1,)), dma((ncomp - 1,)),
            dma((ncomp - 1, ncomp)), dma((ncomp - 1, ncomp)),
            dma((npts - 1,)), dma((npts - 1,)),
            dma((pieces,)), dma((pieces,)),
            dma((pieces,)), dma((pieces,)),
            dma((ngroups - 1, pieces)), dma((ngroups - 1, pieces)),
        ],
        compiler_params=pltpu.CompilerParams(
            collective_id=0, has_side_effects=True, vmem_limit_bytes=60 * 1024 * 1024
        ),
        name="em_step",
    )(
        points, candidates.T, means, variances.reshape(1, owned), log_weights.reshape(1, owned)
    )
    loglik, new_means, new_var, new_logw = pl.pallas_call(
        functools.partial(update_kernel, rows * ncomp * npts, owned * ncomp),
        out_shape=(
            jax.ShapeDtypeStruct((1, rows), f32),
            jax.ShapeDtypeStruct((share, width), f32),
            jax.ShapeDtypeStruct((1, share), f32),
            jax.ShapeDtypeStruct((1, share), f32),
        ),
        in_specs=[vmem, vmem, vmem, anywhere, vmem],
        out_specs=(vmem, vmem, vmem, vmem),
        scratch_shapes=[pltpu.VMEM((share, width), bf16), dma],
        compiler_params=pltpu.CompilerParams(vmem_limit_bytes=60 * 1024 * 1024),
        name="update",
    )(loglik, wsum, sums, means.reshape(npts, share, width), variances.reshape(1, owned))
    return (
        loglik.reshape(rows),
        new_means.reshape(1, share, width),
        new_var,
        new_logw,
    )


def solution(mesh):
    return jax.shard_map(
        functools.partial(on_device, mesh.shape["comp"], mesh.shape["pts"]),
        mesh=mesh,
        in_specs=(
            P(("pts", "comp"), None),
            P(("pts", "comp"), None),
            P("comp", None),
            P("comp"),
            P("comp"),
        ),
        out_specs=(P(("pts", "comp")), P("comp", "pts", None), P("comp", "pts"), P("comp", "pts")),
        check_vma=False,
    )
```

```python
import functools
import math

import jax
import jax.numpy as jnp
from jax import lax
from jax.experimental import pallas as pl
from jax.experimental.pallas import tpu as pltpu
from jax.sharding import PartitionSpec as P

MESH = pl.DeviceIdType.MESH
LANES = 128
LOW = -3.0e38


def em_kernel(
    ncomp, npts, pieces,
    points_ref, cand_ref, means_ref, var_ref, logw_ref,
    loglik_ref, wsum_ref, sums_ref,
    gathered, means, cands, var_row, logw_row, aux, partial, logp, stats, logliks, resp16, sums,
    wsend, land0, kept, relay1, land1, total, relay2, land2,
    load_sem, y_send, y_recv, sib_send, sib_recv, fwd_send, fwd_recv,
    aux_send, aux_recv, st_send, st_recv, sum_send, sum_recv,
    send0, recv0, send1, recv1, send2, recv2,
):
    here_c, here_p = lax.axis_index("comp"), lax.axis_index("pts")
    ny, ngroups = ncomp // 2, npts // 4
    rows, width = points_ref.shape
    owned = means_ref.shape[0]
    block = owned // 2
    share = owned // npts
    piece = width // pieces
    ncand = cand_ref.shape[0]
    y, core = here_c // 2, here_c % 2
    other_core = 1 - core
    sibling = y * 2 + other_core
    group = here_p // 4
    bits = (here_p % 2, (here_p // 2) % 2)
    partners = (here_p + 1 - 2 * bits[0], here_p + 2 - 4 * bits[1])

    def order(c):
        return (1, 0) if c == 1 else (0, 1)

    barrier = pltpu.get_barrier_semaphore()
    for k in range(1, ncomp):
        pl.semaphore_signal(
            barrier, inc=1, device_id=(here_p, (here_c + k) % ncomp), device_id_type=MESH
        )
    for k in range(1, npts):
        pl.semaphore_signal(
            barrier, inc=1, device_id=((here_p + k) % npts, here_c), device_id_type=MESH
        )

    loads = [
        pltpu.make_async_copy(src, dst, load_sem.at[i])
        for i, (src, dst) in enumerate(
            [(cand_ref, cands)]
            + [
                (points_ref.at[:, pl.ds(c * piece, piece)], gathered.at[c, here_c])
                for c in range(pieces)
            ]
            + [(means_ref, means), (var_ref, var_row), (logw_ref, logw_row)]
        )
    ]
    for load in loads:
        load.start()

    for load in loads[: pieces + 1]:
        load.wait()

    def add_point_squares(c, acc):
        for j in range(piece // LANES):
            x = gathered[c, here_c, :, j * LANES : (j + 1) * LANES].astype(jnp.float32)
            acc = acc + x * x
        return acc

    sq = lax.fori_loop(0, pieces, add_point_squares, jnp.zeros((rows, LANES), jnp.float32))
    xx_row = jnp.sum(sq.T, axis=0, keepdims=True)
    aux[here_c] = jnp.concatenate(
        [cands[...].astype(jnp.float32), xx_row]
        + [jnp.zeros((aux.shape[1] - ncand - 1, rows), jnp.float32)],
        axis=0,
    )
    pl.semaphore_wait(barrier, ncomp + npts - 2)

    sends = []

    def send(src, dst, s_sem, r_sem, device):
        copy = pltpu.make_async_remote_copy(
            src_ref=src, dst_ref=dst, send_sem=s_sem, recv_sem=r_sem,
            device_id=device, device_id_type=MESH,
        )
        copy.start()
        sends.append(copy)

    def arrived(dst, s_sem, r_sem):
        pltpu.make_async_remote_copy(
            src_ref=dst, dst_ref=dst, send_sem=s_sem, recv_sem=r_sem,
            device_id=(here_p, sibling), device_id_type=MESH,
        ).wait_recv()

    def part(slot, c):
        return gathered.at[c, slot]

    for c in range(pieces):
        for k in range(1, ny):
            send(part(here_c, c), part(here_c, c), y_send.at[k - 1, c], y_recv.at[k - 1, c],
                 (here_p, ((y + k) % ny) * 2 + core))
        send(part(here_c, c), part(here_c, c), sib_send.at[c], sib_recv.at[c], (here_p, sibling))
        if c == 0:
            for k in range(1, ncomp):
                send(aux.at[here_c], aux.at[here_c], aux_send.at[k - 1], aux_recv.at[k - 1],
                     (here_p, (here_c + k) % ncomp))
    for load in loads[pieces + 1 :]:
        load.wait()

    def pair_dot(chip, c):
        rows2 = gathered[c, pl.ds(2 * chip, 2)].reshape(2 * rows, piece)
        return lax.dot_general(
            means[:, pl.ds(c * piece, piece)], rows2,
            (((1,), (1,)), ((), ())), preferred_element_type=jnp.float32,
        )

    def add_mean_squares(j, acc):
        x = means[:, pl.ds(pl.multiple_of(j * LANES, LANES), LANES)].astype(jnp.float32)
        return acc + x * x

    sq = lax.fori_loop(
        0, width // LANES, add_mean_squares, jnp.zeros((owned, LANES), jnp.float32)
    )
    mm = jnp.sum(sq, axis=1, keepdims=True)
    eye_k = lax.broadcasted_iota(jnp.int32, (owned, owned), 0) == lax.broadcasted_iota(
        jnp.int32, (owned, owned), 1
    )
    var = jnp.sum(jnp.where(eye_k, var_row[...], 0.0), axis=1, keepdims=True)
    logw = jnp.sum(jnp.where(eye_k, logw_row[...], 0.0), axis=1, keepdims=True)
    const = logw - 0.5 * width * jnp.log(2.0 * math.pi * var)
    two_var = 2.0 * var

    def named(s, b):
        number = (here_c * 2 + b).astype(jnp.float32)
        hit = aux[s, 0:1, :] == number
        for j in range(1, ncand):
            hit = hit | (aux[s, j : j + 1, :] == number)
        return hit

    def finish(s, g):
        xx = aux[s, ncand : ncand + 1, :]
        lp = const - (xx - 2.0 * g + mm) / two_var
        logp[s] = lp
        tops, totals = [], []
        for b in range(2):
            half = lp[b * block : (b + 1) * block]
            top = jnp.max(half, axis=0, keepdims=True)
            hit = named(s, b)
            part_sum = jnp.sum(jnp.exp(half - top), axis=0, keepdims=True)
            tops.append(jnp.where(hit, top, LOW))
            totals.append(jnp.where(hit, part_sum, 0.0))
        top = jnp.maximum(tops[0], tops[1])
        stats[here_c, s, 0:1, :] = top
        stats[here_c, s, 1:2, :] = totals[0] * jnp.exp(tops[0] - top) + totals[1] * jnp.exp(
            tops[1] - top
        )
        for k in range(1, ncomp):
            send(stats.at[here_c, s], stats.at[here_c, s], st_send.at[k - 1, s],
                 st_recv.at[k - 1, s], (here_p, (here_c + k) % ncomp))

    def add_pair(chip, c):
        g = pair_dot(chip, c)
        if c:
            g = partial[chip] + g
        if c < pieces - 1:
            partial[chip] = g
        else:
            for j in range(2):
                finish(2 * chip + j, g[:, j * rows : (j + 1) * rows])

    def take_forwarded(c):
        for k in range(1, ny):
            chip = (y + ny - k) % ny
            arrived(part(chip * 2 + other_core, c), fwd_send.at[k - 1, c], fwd_recv.at[k - 1, c])
            add_pair(chip, c)

    own = 0
    for c in range(pieces):
        for k in range(1, ny):
            slot = ((y + ny - k) % ny) * 2 + core
            arrived(part(slot, c), y_send.at[k - 1, c], y_recv.at[k - 1, c])
            send(part(slot, c), part(slot, c), fwd_send.at[k - 1, c], fwd_recv.at[k - 1, c],
                 (here_p, sibling))
        if c == 0:
            for k in range(1, ncomp):
                arrived(aux.at[(here_c + ncomp - k) % ncomp], aux_send.at[k - 1],
                        aux_recv.at[k - 1])
        for _ in range(2):
            if own < pieces:
                arrived(part(sibling, own), sib_send.at[own], sib_recv.at[own])
                add_pair(y, own)
                own += 1
        if c:
            take_forwarded(c - 1)
    take_forwarded(pieces - 1)

    for k in range(1, ncomp):
        owner = (here_c + ncomp - k) % ncomp
        for s in range(ncomp):
            arrived(stats.at[owner, s], st_send.at[k - 1, s], st_recv.at[k - 1, s])

    count_sum = [jnp.zeros((block, rows), jnp.float32) for _ in range(2)]
    sq_sum = [jnp.zeros((block, rows), jnp.float32) for _ in range(2)]
    for s in range(ncomp):
        lanes = slice(s * rows, (s + 1) * rows)
        tops = [stats[o, s, 0:1, :] for o in range(ncomp)]
        top = functools.reduce(jnp.maximum, tops)
        weight = stats[0, s, 1:2, :] * jnp.exp(tops[0] - top)
        for o in range(1, ncomp):
            weight = weight + stats[o, s, 1:2, :] * jnp.exp(tops[o] - top)
        loglik = top + jnp.log(weight)
        logliks[s] = loglik
        xx = aux[s, ncand : ncand + 1, :]
        for b in range(2):
            resp = jnp.where(
                named(s, b), jnp.exp(logp[s, b * block : (b + 1) * block, :] - loglik), 0.0
            )
            resp16[b * block : (b + 1) * block, lanes] = resp.astype(jnp.bfloat16)
            count_sum[b] = count_sum[b] + resp
            sq_sum[b] = sq_sum[b] + resp * xx

    def make(c):
        data = gathered[c].reshape(ncomp * rows, piece)
        w = jnp.dot(resp16[...], data, preferred_element_type=jnp.float32)
        first, second = order(c)
        for g in range(ngroups):
            for n in range(4):
                dest = (n % 2, n // 2)
                start = (g * 4 + n) * share
                wsend[c, dest[first], dest[second], g] = w[start : start + share].astype(
                    jnp.bfloat16
                )
        send(wsend.at[c, 1 - bits[first]], land0.at[c], send0.at[c], recv0.at[c],
             (partners[first], here_c))

    def halve(c):
        first, second = order(c)
        mine, other = bits[second], 1 - bits[second]
        arrived(land0.at[c], send0.at[c], recv0.at[c])
        relay1[c] = (
            wsend[c, bits[first], other].astype(jnp.float32) + land0[c, other].astype(jnp.float32)
        ).astype(jnp.bfloat16)
        send(relay1.at[c], land1.at[c], send1.at[c], recv1.at[c], (partners[second], here_c))
        kept[c] = wsend[c, bits[first], mine].astype(jnp.float32) + land0[c, mine].astype(
            jnp.float32
        )

    def spread(c):
        arrived(land1.at[c], send1.at[c], recv1.at[c])
        both = kept[c] + land1[c].astype(jnp.float32)
        relay2[c] = both.astype(jnp.bfloat16)
        for k in range(1, ngroups):
            to = (group + k) % ngroups
            send(relay2.at[c, to], land2.at[k - 1, c], send2.at[k - 1, c], recv2.at[k - 1, c],
                 (to * 4 + here_p % 4, here_c))
        total[c] = both

    def share_sums():
        loglik_ref[...] = logliks[here_c]
        for b in range(2):
            cols = slice(b * block, (b + 1) * block)
            sums[0, 0:1, cols] = jnp.sum(count_sum[b].T, axis=0, keepdims=True)
            sums[0, 1:2, cols] = jnp.sum(sq_sum[b].T, axis=0, keepdims=True)
        for k in range(1, npts):
            send(sums.at[0], sums.at[k], sum_send.at[k - 1], sum_recv.at[k - 1],
                 ((here_p + k) % npts, here_c))

    def take_sums():
        for k in range(1, npts):
            arrived(sums.at[k], sum_send.at[k - 1], sum_recv.at[k - 1])
        both = sums[0]
        for k in range(1, npts):
            both = both + sums[k]
        sums_ref[...] = both

    lag = 2
    for t in range(pieces + lag + 2):
        if t < pieces:
            make(t)
        if t == 1:
            share_sums()
        if lag <= t < pieces + lag:
            halve(t - lag)
        if lag < t <= pieces + lag:
            spread(t - lag - 1)
        if t == pieces:
            take_sums()
        if t >= lag + 2:
            c = t - lag - 2
            w = total[c, group]
            for k in range(1, ngroups):
                arrived(land2.at[k - 1, c], send2.at[k - 1, c], recv2.at[k - 1, c])
                w = w + land2[k - 1, c].astype(jnp.float32)
            wsum_ref[:, c * piece : (c + 1) * piece] = w

    for copy in sends:
        copy.wait_send()


def update_kernel(
    npoints, ncomponents,
    loglik_ref, wsum_ref, sums_ref, shares_ref, var_ref,
    loglik_out, mean_ref, newvar_ref, newlogw_ref,
    mu_old, load_sem,
):
    here_p = lax.axis_index("pts")
    load = pltpu.make_async_copy(shares_ref.at[here_p], mu_old, load_sem)
    load.start()
    share, width = wsum_ref.shape
    owned = sums_ref.shape[1]
    mine = lax.broadcasted_iota(jnp.int32, (share, owned), 1) == (
        lax.broadcasted_iota(jnp.int32, (share, owned), 0) + here_p * share
    )

    def column(row):
        return jnp.sum(jnp.where(mine, row, 0.0), axis=1, keepdims=True)

    loglik_out[...] = loglik_ref[...]
    counts, sqsum = column(sums_ref[0:1, :]), column(sums_ref[1:2, :])
    var_old = column(var_ref[...])
    scale = 1.0 / (counts + 1.0)
    cross = jnp.zeros((share, LANES), jnp.float32)
    norm = jnp.zeros((share, LANES), jnp.float32)
    load.wait()
    for j in range(width // LANES):
        cols = slice(j * LANES, (j + 1) * LANES)
        w = wsum_ref[:, cols]
        new = (w + mu_old[:, cols].astype(jnp.float32)) * scale
        mean_ref[:, cols] = new
        cross = cross + new * w
        norm = norm + new * new
    cross = jnp.sum(cross, axis=1, keepdims=True)
    norm = jnp.sum(norm, axis=1, keepdims=True)
    resid = sqsum - 2.0 * cross + counts * norm + width * var_old
    new_var = resid / (width * (counts + 1.0))
    new_logw = jnp.log((counts + 1.0) / float(npoints + ncomponents))
    eye = lax.broadcasted_iota(jnp.int32, (share, share), 0) == lax.broadcasted_iota(
        jnp.int32, (share, share), 1
    )
    newvar_ref[...] = jnp.sum(jnp.where(eye, new_var, 0.0), axis=0, keepdims=True)
    newlogw_ref[...] = jnp.sum(jnp.where(eye, new_logw, 0.0), axis=0, keepdims=True)


def on_device(ncomp, npts, points, candidates, means, variances, log_weights):
    rows, width = points.shape
    owned = means.shape[0]
    share = owned // npts
    ngroups = npts // 4
    pieces = 6
    ncand = candidates.shape[1]
    ny = ncomp // 2
    aux_rows = -(-(ncand + 1) // 8) * 8
    f32, bf16 = jnp.float32, jnp.bfloat16
    dma = pltpu.SemaphoreType.DMA
    vmem = pl.BlockSpec(memory_space=pltpu.VMEM)
    anywhere = pl.BlockSpec(memory_space=pl.ANY)
    piece = width // pieces
    loglik, wsum, sums = pl.pallas_call(
        functools.partial(em_kernel, ncomp, npts, pieces),
        out_shape=(
            jax.ShapeDtypeStruct((1, rows), f32),
            jax.ShapeDtypeStruct((share, width), f32),
            jax.ShapeDtypeStruct((2, owned), f32),
        ),
        in_specs=[anywhere] * 5,
        out_specs=(vmem, vmem, vmem),
        scratch_shapes=[
            pltpu.VMEM((pieces, ncomp, rows, piece), bf16),
            pltpu.VMEM((owned, width), bf16),
            pltpu.VMEM((ncand, rows), jnp.int32),
            pltpu.VMEM((1, owned), f32),
            pltpu.VMEM((1, owned), f32),
            pltpu.VMEM((ncomp, aux_rows, rows), f32),
            pltpu.VMEM((ny, owned, 2 * rows), f32),
            pltpu.VMEM((ncomp, owned, rows), f32),
            pltpu.VMEM((ncomp, ncomp, 2, rows), f32),
            pltpu.VMEM((ncomp, 1, rows), f32),
            pltpu.VMEM((owned, ncomp * rows), bf16),
            pltpu.VMEM((npts, 2, owned), f32),
            pltpu.VMEM((pieces, 2, 2, ngroups, share, piece), bf16),
            pltpu.VMEM((pieces, 2, ngroups, share, piece), bf16),
            pltpu.VMEM((pieces, ngroups, share, piece), f32),
            pltpu.VMEM((pieces, ngroups, share, piece), bf16),
            pltpu.VMEM((pieces, ngroups, share, piece), bf16),
            pltpu.VMEM((pieces, ngroups, share, piece), f32),
            pltpu.VMEM((pieces, ngroups, share, piece), bf16),
            pltpu.VMEM((ngroups - 1, pieces, share, piece), bf16),
            dma((pieces + 4,)),
            dma((ny - 1, pieces)), dma((ny - 1, pieces)),
            dma((pieces,)), dma((pieces,)),
            dma((ny - 1, pieces)), dma((ny - 1, pieces)),
            dma((ncomp - 1,)), dma((ncomp - 1,)),
            dma((ncomp - 1, ncomp)), dma((ncomp - 1, ncomp)),
            dma((npts - 1,)), dma((npts - 1,)),
            dma((pieces,)), dma((pieces,)),
            dma((pieces,)), dma((pieces,)),
            dma((ngroups - 1, pieces)), dma((ngroups - 1, pieces)),
        ],
        compiler_params=pltpu.CompilerParams(
            collective_id=0, has_side_effects=True, vmem_limit_bytes=60 * 1024 * 1024
        ),
        name="em_step",
    )(
        points, candidates.T, means, variances.reshape(1, owned), log_weights.reshape(1, owned)
    )
    loglik, new_means, new_var, new_logw = pl.pallas_call(
        functools.partial(update_kernel, rows * ncomp * npts, owned * ncomp),
        out_shape=(
            jax.ShapeDtypeStruct((1, rows), f32),
            jax.ShapeDtypeStruct((share, width), f32),
            jax.ShapeDtypeStruct((1, share), f32),
            jax.ShapeDtypeStruct((1, share), f32),
        ),
        in_specs=[vmem, vmem, vmem, anywhere, vmem],
        out_specs=(vmem, vmem, vmem, vmem),
        scratch_shapes=[pltpu.VMEM((share, width), bf16), dma],
        compiler_params=pltpu.CompilerParams(vmem_limit_bytes=60 * 1024 * 1024),
        name="update",
    )(loglik, wsum, sums, means.reshape(npts, share, width), variances.reshape(1, owned))
    return (
        loglik.reshape(rows),
        new_means.reshape(1, share, width),
        new_var,
        new_logw,
    )


def solution(mesh):
    return jax.shard_map(
        functools.partial(on_device, mesh.shape["comp"], mesh.shape["pts"]),
        mesh=mesh,
        in_specs=(
            P(("pts", "comp"), None),
            P(("pts", "comp"), None),
            P("comp", None),
            P("comp"),
            P("comp"),
        ),
        out_specs=(P(("pts", "comp")), P("comp", "pts", None), P("comp", "pts"), P("comp", "pts")),
        check_vma=False,
    )
```

```python
import functools
import math

import jax
import jax.numpy as jnp
from jax import lax
from jax.experimental import pallas as pl
from jax.experimental.pallas import tpu as pltpu
from jax.sharding import PartitionSpec as P

MESH = pl.DeviceIdType.MESH
LANES = 128
LOW = -3.0e38


def em_kernel(
    ncomp, npts, pieces,
    points_ref, cand_ref, means_ref, var_ref, logw_ref,
    loglik_ref, wsum_ref, sums_ref,
    gathered, means, cands, var_row, logw_row, aux, partial, logp, stats, logliks, resp16, sums,
    wsend, land0, kept, relay1, land1, total, relay2, land2,
    load_sem, y_send, y_recv, sib_send, sib_recv, fwd_send, fwd_recv,
    aux_send, aux_recv, st_send, st_recv, sum_send, sum_recv,
    send0, recv0, send1, recv1, send2, recv2,
):
    here_c, here_p = lax.axis_index("comp"), lax.axis_index("pts")
    ny, ngroups = ncomp // 2, npts // 4
    rows, width = points_ref.shape
    owned = means_ref.shape[0]
    block = owned // 2
    share = owned // npts
    piece = width // pieces
    ncand = cand_ref.shape[0]
    y, core = here_c // 2, here_c % 2
    other_core = 1 - core
    sibling = y * 2 + other_core
    group = here_p // 4
    bit0, bit1 = here_p % 2, (here_p // 2) % 2
    bits = (bit0 + core * (bit1 - bit0), bit1 + core * (bit0 - bit1))
    strides = (1 + core, 2 - core)
    partners = tuple(here_p + (1 - 2 * bit) * stride for bit, stride in zip(bits, strides))

    barrier = pltpu.get_barrier_semaphore()
    for k in range(1, ncomp):
        pl.semaphore_signal(
            barrier, inc=1, device_id=(here_p, (here_c + k) % ncomp), device_id_type=MESH
        )
    for k in range(1, npts):
        pl.semaphore_signal(
            barrier, inc=1, device_id=((here_p + k) % npts, here_c), device_id_type=MESH
        )

    loads = [
        pltpu.make_async_copy(src, dst, load_sem.at[i])
        for i, (src, dst) in enumerate(
            [(cand_ref, cands)]
            + [
                (points_ref.at[:, pl.ds(c * piece, piece)], gathered.at[c, here_c])
                for c in range(pieces)
            ]
            + [(means_ref, means), (var_ref, var_row), (logw_ref, logw_row)]
        )
    ]
    for load in loads:
        load.start()

    for load in loads[: pieces + 1]:
        load.wait()

    def add_point_squares(c, acc):
        for j in range(piece // LANES):
            x = gathered[c, here_c, :, j * LANES : (j + 1) * LANES].astype(jnp.float32)
            acc = acc + x * x
        return acc

    sq = lax.fori_loop(0, pieces, add_point_squares, jnp.zeros((rows, LANES), jnp.float32))
    xx_row = jnp.sum(sq.T, axis=0, keepdims=True)
    aux[here_c] = jnp.concatenate(
        [cands[...].astype(jnp.float32), xx_row]
        + [jnp.zeros((aux.shape[1] - ncand - 1, rows), jnp.float32)],
        axis=0,
    )
    pl.semaphore_wait(barrier, ncomp + npts - 2)

    sends = []

    def send(src, dst, s_sem, r_sem, device):
        copy = pltpu.make_async_remote_copy(
            src_ref=src, dst_ref=dst, send_sem=s_sem, recv_sem=r_sem,
            device_id=device, device_id_type=MESH,
        )
        copy.start()
        sends.append(copy)

    def arrived(dst, s_sem, r_sem):
        pltpu.make_async_remote_copy(
            src_ref=dst, dst_ref=dst, send_sem=s_sem, recv_sem=r_sem,
            device_id=(here_p, sibling), device_id_type=MESH,
        ).wait_recv()

    def part(slot, c):
        return gathered.at[c, slot]

    def send_y(c):
        for k in range(1, ny):
            send(part(here_c, c), part(here_c, c), y_send.at[k - 1, c], y_recv.at[k - 1, c],
                 (here_p, ((y + k) % ny) * 2 + core))

    def send_sibling(c):
        send(part(here_c, c), part(here_c, c), sib_send.at[c], sib_recv.at[c], (here_p, sibling))

    ahead = 2
    for c in range(ahead):
        send_y(c)
        send_sibling(c)
        if c == 0:
            for k in range(1, ncomp):
                send(aux.at[here_c], aux.at[here_c], aux_send.at[k - 1], aux_recv.at[k - 1],
                     (here_p, (here_c + k) % ncomp))

    for load in loads[pieces + 1 :]:
        load.wait()

    def pair_dot(chip, c):
        rows2 = gathered[c, pl.ds(2 * chip, 2)].reshape(2 * rows, piece)
        return lax.dot_general(
            means[:, pl.ds(c * piece, piece)], rows2,
            (((1,), (1,)), ((), ())), preferred_element_type=jnp.float32,
        )

    def add_mean_squares(j, acc):
        x = means[:, pl.ds(pl.multiple_of(j * LANES, LANES), LANES)].astype(jnp.float32)
        return acc + x * x

    sq = lax.fori_loop(
        0, width // LANES, add_mean_squares, jnp.zeros((owned, LANES), jnp.float32)
    )
    mm = jnp.sum(sq, axis=1, keepdims=True)
    eye_k = lax.broadcasted_iota(jnp.int32, (owned, owned), 0) == lax.broadcasted_iota(
        jnp.int32, (owned, owned), 1
    )
    var = jnp.sum(jnp.where(eye_k, var_row[...], 0.0), axis=1, keepdims=True)
    logw = jnp.sum(jnp.where(eye_k, logw_row[...], 0.0), axis=1, keepdims=True)
    const = logw - 0.5 * width * jnp.log(2.0 * math.pi * var)
    two_var = 2.0 * var

    def named(s, b):
        number = (here_c * 2 + b).astype(jnp.float32)
        hit = aux[s, 0:1, :] == number
        for j in range(1, ncand):
            hit = hit | (aux[s, j : j + 1, :] == number)
        return hit

    def finish(s, g):
        xx = aux[s, ncand : ncand + 1, :]
        lp = const - (xx - 2.0 * g + mm) / two_var
        logp[s] = lp
        tops, totals = [], []
        for b in range(2):
            half = lp[b * block : (b + 1) * block]
            top = jnp.max(half, axis=0, keepdims=True)
            hit = named(s, b)
            part_sum = jnp.sum(jnp.exp(half - top), axis=0, keepdims=True)
            tops.append(jnp.where(hit, top, LOW))
            totals.append(jnp.where(hit, part_sum, 0.0))
        top = jnp.maximum(tops[0], tops[1])
        stats[here_c, s, 0:1, :] = top
        stats[here_c, s, 1:2, :] = totals[0] * jnp.exp(tops[0] - top) + totals[1] * jnp.exp(
            tops[1] - top
        )
        for k in range(1, ncomp):
            send(stats.at[here_c, s], stats.at[here_c, s], st_send.at[k - 1, s],
                 st_recv.at[k - 1, s], (here_p, (here_c + k) % ncomp))

    def add_pair(chip, c):
        g = pair_dot(chip, c)
        if c:
            g = partial[chip] + g
        if c < pieces - 1:
            partial[chip] = g
        else:
            for j in range(2):
                finish(2 * chip + j, g[:, j * rows : (j + 1) * rows])

    def take_forwarded(c):
        for k in range(1, ny):
            chip = (y + ny - k) % ny
            arrived(part(chip * 2 + other_core, c), fwd_send.at[k - 1, c], fwd_recv.at[k - 1, c])
            add_pair(chip, c)

    own = 0
    for c in range(pieces):
        for k in range(1, ny):
            slot = ((y + ny - k) % ny) * 2 + core
            arrived(part(slot, c), y_send.at[k - 1, c], y_recv.at[k - 1, c])
            send(part(slot, c), part(slot, c), fwd_send.at[k - 1, c], fwd_recv.at[k - 1, c],
                 (here_p, sibling))
        if c + ahead < pieces:
            send_y(c + ahead)
        for n in range(ahead + 2 * c, min(pieces, ahead + 2 * c + 2)):
            send_sibling(n)
        if c == 0:
            for k in range(1, ncomp):
                arrived(aux.at[(here_c + ncomp - k) % ncomp], aux_send.at[k - 1],
                        aux_recv.at[k - 1])
        for _ in range(2):
            if own < pieces:
                arrived(part(sibling, own), sib_send.at[own], sib_recv.at[own])
                add_pair(y, own)
                own += 1
        if c:
            take_forwarded(c - 1)
    take_forwarded(pieces - 1)

    for k in range(1, ncomp):
        owner = (here_c + ncomp - k) % ncomp
        for s in range(ncomp):
            arrived(stats.at[owner, s], st_send.at[k - 1, s], st_recv.at[k - 1, s])

    count_sum = [jnp.zeros((block, rows), jnp.float32) for _ in range(2)]
    sq_sum = [jnp.zeros((block, rows), jnp.float32) for _ in range(2)]
    for s in range(ncomp):
        lanes = slice(s * rows, (s + 1) * rows)
        tops = [stats[o, s, 0:1, :] for o in range(ncomp)]
        top = functools.reduce(jnp.maximum, tops)
        weight = stats[0, s, 1:2, :] * jnp.exp(tops[0] - top)
        for o in range(1, ncomp):
            weight = weight + stats[o, s, 1:2, :] * jnp.exp(tops[o] - top)
        loglik = top + jnp.log(weight)
        logliks[s] = loglik
        xx = aux[s, ncand : ncand + 1, :]
        for b in range(2):
            resp = jnp.where(
                named(s, b), jnp.exp(logp[s, b * block : (b + 1) * block, :] - loglik), 0.0
            )
            resp16[b * block : (b + 1) * block, lanes] = resp.astype(jnp.bfloat16)
            count_sum[b] = count_sum[b] + resp
            sq_sum[b] = sq_sum[b] + resp * xx

    def make(c):
        data = gathered[c].reshape(ncomp * rows, piece)
        w = jnp.dot(resp16[...], data, preferred_element_type=jnp.float32)
        for g in range(ngroups):
            for n in range(4):
                lo, hi = n % 2, n // 2
                start = (g * 4 + n) * share
                wsend[c, lo + core * (hi - lo), hi + core * (lo - hi), g] = w[
                    start : start + share
                ].astype(jnp.bfloat16)
        send(wsend.at[c, 1 - bits[0]], land0.at[c], send0.at[c], recv0.at[c],
             (partners[0], here_c))

    def halve(c):
        mine, other = bits[1], 1 - bits[1]
        arrived(land0.at[c], send0.at[c], recv0.at[c])
        relay1[c] = (
            wsend[c, bits[0], other].astype(jnp.float32) + land0[c, other].astype(jnp.float32)
        ).astype(jnp.bfloat16)
        send(relay1.at[c], land1.at[c], send1.at[c], recv1.at[c], (partners[1], here_c))
        kept[c] = wsend[c, bits[0], mine].astype(jnp.float32) + land0[c, mine].astype(
            jnp.float32
        )

    def spread(c):
        arrived(land1.at[c], send1.at[c], recv1.at[c])
        both = kept[c] + land1[c].astype(jnp.float32)
        relay2[c] = both.astype(jnp.bfloat16)
        for k in range(1, ngroups):
            to = (group + k) % ngroups
            send(relay2.at[c, to], land2.at[k - 1, c], send2.at[k - 1, c], recv2.at[k - 1, c],
                 (to * 4 + here_p % 4, here_c))
        total[c] = both

    def share_sums():
        loglik_ref[...] = logliks[here_c]
        for b in range(2):
            cols = slice(b * block, (b + 1) * block)
            sums[0, 0:1, cols] = jnp.sum(count_sum[b].T, axis=0, keepdims=True)
            sums[0, 1:2, cols] = jnp.sum(sq_sum[b].T, axis=0, keepdims=True)
        for k in range(1, npts):
            send(sums.at[0], sums.at[k], sum_send.at[k - 1], sum_recv.at[k - 1],
                 ((here_p + k) % npts, here_c))

    def take_sums():
        for k in range(1, npts):
            arrived(sums.at[k], sum_send.at[k - 1], sum_recv.at[k - 1])
        both = sums[0]
        for k in range(1, npts):
            both = both + sums[k]
        sums_ref[...] = both

    lag = 2
    for t in range(pieces + lag + 2):
        if t < pieces:
            make(t)
        if t == 1:
            share_sums()
        if lag <= t < pieces + lag:
            halve(t - lag)
        if lag < t <= pieces + lag:
            spread(t - lag - 1)
        if t == pieces:
            take_sums()
        if t >= lag + 2:
            c = t - lag - 2
            w = total[c, group]
            for k in range(1, ngroups):
                arrived(land2.at[k - 1, c], send2.at[k - 1, c], recv2.at[k - 1, c])
                w = w + land2[k - 1, c].astype(jnp.float32)
            wsum_ref[:, c * piece : (c + 1) * piece] = w

    for copy in sends:
        copy.wait_send()


def update_kernel(
    npoints, ncomponents,
    loglik_ref, wsum_ref, sums_ref, shares_ref, var_ref,
    loglik_out, mean_ref, newvar_ref, newlogw_ref,
    mu_old, load_sem,
):
    here_p = lax.axis_index("pts")
    load = pltpu.make_async_copy(shares_ref.at[here_p], mu_old, load_sem)
    load.start()
    share, width = wsum_ref.shape
    owned = sums_ref.shape[1]
    mine = lax.broadcasted_iota(jnp.int32, (share, owned), 1) == (
        lax.broadcasted_iota(jnp.int32, (share, owned), 0) + here_p * share
    )

    def column(row):
        return jnp.sum(jnp.where(mine, row, 0.0), axis=1, keepdims=True)

    loglik_out[...] = loglik_ref[...]
    counts, sqsum = column(sums_ref[0:1, :]), column(sums_ref[1:2, :])
    var_old = column(var_ref[...])
    scale = 1.0 / (counts + 1.0)
    cross = jnp.zeros((share, LANES), jnp.float32)
    norm = jnp.zeros((share, LANES), jnp.float32)
    load.wait()
    for j in range(width // LANES):
        cols = slice(j * LANES, (j + 1) * LANES)
        w = wsum_ref[:, cols]
        new = (w + mu_old[:, cols].astype(jnp.float32)) * scale
        mean_ref[:, cols] = new
        cross = cross + new * w
        norm = norm + new * new
    cross = jnp.sum(cross, axis=1, keepdims=True)
    norm = jnp.sum(norm, axis=1, keepdims=True)
    resid = sqsum - 2.0 * cross + counts * norm + width * var_old
    new_var = resid / (width * (counts + 1.0))
    new_logw = jnp.log((counts + 1.0) / float(npoints + ncomponents))
    eye = lax.broadcasted_iota(jnp.int32, (share, share), 0) == lax.broadcasted_iota(
        jnp.int32, (share, share), 1
    )
    newvar_ref[...] = jnp.sum(jnp.where(eye, new_var, 0.0), axis=0, keepdims=True)
    newlogw_ref[...] = jnp.sum(jnp.where(eye, new_logw, 0.0), axis=0, keepdims=True)


def on_device(ncomp, npts, points, candidates, means, variances, log_weights):
    rows, width = points.shape
    owned = means.shape[0]
    share = owned // npts
    ngroups = npts // 4
    pieces = 6
    ncand = candidates.shape[1]
    ny = ncomp // 2
    aux_rows = -(-(ncand + 1) // 8) * 8
    f32, bf16 = jnp.float32, jnp.bfloat16
    dma = pltpu.SemaphoreType.DMA
    vmem = pl.BlockSpec(memory_space=pltpu.VMEM)
    anywhere = pl.BlockSpec(memory_space=pl.ANY)
    piece = width // pieces
    loglik, wsum, sums = pl.pallas_call(
        functools.partial(em_kernel, ncomp, npts, pieces),
        out_shape=(
            jax.ShapeDtypeStruct((1, rows), f32),
            jax.ShapeDtypeStruct((share, width), f32),
            jax.ShapeDtypeStruct((2, owned), f32),
        ),
        in_specs=[anywhere] * 5,
        out_specs=(vmem, vmem, vmem),
        scratch_shapes=[
            pltpu.VMEM((pieces, ncomp, rows, piece), bf16),
            pltpu.VMEM((owned, width), bf16),
            pltpu.VMEM((ncand, rows), jnp.int32),
            pltpu.VMEM((1, owned), f32),
            pltpu.VMEM((1, owned), f32),
            pltpu.VMEM((ncomp, aux_rows, rows), f32),
            pltpu.VMEM((ny, owned, 2 * rows), f32),
            pltpu.VMEM((ncomp, owned, rows), f32),
            pltpu.VMEM((ncomp, ncomp, 2, rows), f32),
            pltpu.VMEM((ncomp, 1, rows), f32),
            pltpu.VMEM((owned, ncomp * rows), bf16),
            pltpu.VMEM((npts, 2, owned), f32),
            pltpu.VMEM((pieces, 2, 2, ngroups, share, piece), bf16),
            pltpu.VMEM((pieces, 2, ngroups, share, piece), bf16),
            pltpu.VMEM((pieces, ngroups, share, piece), f32),
            pltpu.VMEM((pieces, ngroups, share, piece), bf16),
            pltpu.VMEM((pieces, ngroups, share, piece), bf16),
            pltpu.VMEM((pieces, ngroups, share, piece), f32),
            pltpu.VMEM((pieces, ngroups, share, piece), bf16),
            pltpu.VMEM((ngroups - 1, pieces, share, piece), bf16),
            dma((pieces + 4,)),
            dma((ny - 1, pieces)), dma((ny - 1, pieces)),
            dma((pieces,)), dma((pieces,)),
            dma((ny - 1, pieces)), dma((ny - 1, pieces)),
            dma((ncomp - 1,)), dma((ncomp - 1,)),
            dma((ncomp - 1, ncomp)), dma((ncomp - 1, ncomp)),
            dma((npts - 1,)), dma((npts - 1,)),
            dma((pieces,)), dma((pieces,)),
            dma((pieces,)), dma((pieces,)),
            dma((ngroups - 1, pieces)), dma((ngroups - 1, pieces)),
        ],
        compiler_params=pltpu.CompilerParams(
            collective_id=0, has_side_effects=True, vmem_limit_bytes=60 * 1024 * 1024
        ),
        name="em_step",
    )(
        points, candidates.T, means, variances.reshape(1, owned), log_weights.reshape(1, owned)
    )
    loglik, new_means, new_var, new_logw = pl.pallas_call(
        functools.partial(update_kernel, rows * ncomp * npts, owned * ncomp),
        out_shape=(
            jax.ShapeDtypeStruct((1, rows), f32),
            jax.ShapeDtypeStruct((share, width), f32),
            jax.ShapeDtypeStruct((1, share), f32),
            jax.ShapeDtypeStruct((1, share), f32),
        ),
        in_specs=[vmem, vmem, vmem, anywhere, vmem],
        out_specs=(vmem, vmem, vmem, vmem),
        scratch_shapes=[pltpu.VMEM((share, width), bf16), dma],
        compiler_params=pltpu.CompilerParams(vmem_limit_bytes=60 * 1024 * 1024),
        name="update",
    )(loglik, wsum, sums, means.reshape(npts, share, width), variances.reshape(1, owned))
    return (
        loglik.reshape(rows),
        new_means.reshape(1, share, width),
        new_var,
        new_logw,
    )


def solution(mesh):
    return jax.shard_map(
        functools.partial(on_device, mesh.shape["comp"], mesh.shape["pts"]),
        mesh=mesh,
        in_specs=(
            P(("pts", "comp"), None),
            P(("pts", "comp"), None),
            P("comp", None),
            P("comp"),
            P("comp"),
        ),
        out_specs=(P(("pts", "comp")), P("comp", "pts", None), P("comp", "pts"), P("comp", "pts")),
        check_vma=False,
    )
```

```python
import functools
import math

import jax
import jax.numpy as jnp
from jax import lax
from jax.experimental import pallas as pl
from jax.experimental.pallas import tpu as pltpu
from jax.sharding import PartitionSpec as P

MESH = pl.DeviceIdType.MESH
LANES = 128
LOW = -3.0e38


def em_kernel(
    ncomp, npts, pieces,
    points_ref, cand_ref, means_ref, var_ref, logw_ref,
    loglik_ref, wsum_ref, sums_ref,
    gathered, means, cands, var_row, logw_row, aux, partial, logp, stats, logliks, resp16, sums,
    wsend, land0, kept, relay1, land1, total, relay2, land2, wsum, both_sums,
    load_sem, y_send, y_recv, sib_send, sib_recv, fwd_send, fwd_recv,
    aux_send, aux_recv, st_send, st_recv, sum_send, sum_recv,
    send0, recv0, send1, recv1, send2, recv2, out_sem,
):
    here_c, here_p = lax.axis_index("comp"), lax.axis_index("pts")
    ny, ngroups = ncomp // 2, npts // 4
    rows, width = points_ref.shape
    owned = means_ref.shape[0]
    block = owned // 2
    share = owned // npts
    piece = width // pieces
    ncand = cand_ref.shape[0]
    y, core = here_c // 2, here_c % 2
    other_core = 1 - core
    sibling = y * 2 + other_core
    group = here_p // 4
    bit0, bit1 = here_p % 2, (here_p // 2) % 2
    bits = (bit0 + core * (bit1 - bit0), bit1 + core * (bit0 - bit1))
    strides = (1 + core, 2 - core)
    partners = tuple(here_p + (1 - 2 * bit) * stride for bit, stride in zip(bits, strides))

    barrier = pltpu.get_barrier_semaphore()
    for k in range(1, ncomp):
        pl.semaphore_signal(
            barrier, inc=1, device_id=(here_p, (here_c + k) % ncomp), device_id_type=MESH
        )
    for k in range(1, npts):
        pl.semaphore_signal(
            barrier, inc=1, device_id=((here_p + k) % npts, here_c), device_id_type=MESH
        )

    loads = [
        pltpu.make_async_copy(src, dst, load_sem.at[i])
        for i, (src, dst) in enumerate(
            [(cand_ref, cands)]
            + [
                (points_ref.at[:, pl.ds(c * piece, piece)], gathered.at[c, here_c])
                for c in range(pieces)
            ]
            + [(means_ref, means), (var_ref, var_row), (logw_ref, logw_row)]
        )
    ]
    for load in loads:
        load.start()

    for load in loads[: pieces + 1]:
        load.wait()

    def add_point_squares(c, acc):
        for j in range(piece // LANES):
            x = gathered[c, here_c, :, j * LANES : (j + 1) * LANES].astype(jnp.float32)
            acc = acc + x * x
        return acc

    sq = lax.fori_loop(0, pieces, add_point_squares, jnp.zeros((rows, LANES), jnp.float32))
    xx_row = jnp.sum(sq.T, axis=0, keepdims=True)
    aux[here_c] = jnp.concatenate(
        [cands[...].astype(jnp.float32), xx_row]
        + [jnp.zeros((aux.shape[1] - ncand - 1, rows), jnp.float32)],
        axis=0,
    )
    pl.semaphore_wait(barrier, ncomp + npts - 2)

    sends, stores = [], []

    def store(src, dst, i):
        copy = pltpu.make_async_copy(src, dst, out_sem.at[i])
        copy.start()
        stores.append(copy)

    def send(src, dst, s_sem, r_sem, device):
        copy = pltpu.make_async_remote_copy(
            src_ref=src, dst_ref=dst, send_sem=s_sem, recv_sem=r_sem,
            device_id=device, device_id_type=MESH,
        )
        copy.start()
        sends.append(copy)

    def arrived(dst, s_sem, r_sem):
        pltpu.make_async_remote_copy(
            src_ref=dst, dst_ref=dst, send_sem=s_sem, recv_sem=r_sem,
            device_id=(here_p, sibling), device_id_type=MESH,
        ).wait_recv()

    def part(slot, c):
        return gathered.at[c, slot]

    def send_y(c):
        for k in range(1, ny):
            send(part(here_c, c), part(here_c, c), y_send.at[k - 1, c], y_recv.at[k - 1, c],
                 (here_p, ((y + k) % ny) * 2 + core))

    def send_sibling(c):
        send(part(here_c, c), part(here_c, c), sib_send.at[c], sib_recv.at[c], (here_p, sibling))

    ahead = 2
    for c in range(ahead):
        send_y(c)
        send_sibling(c)
        if c == 0:
            for k in range(1, ncomp):
                send(aux.at[here_c], aux.at[here_c], aux_send.at[k - 1], aux_recv.at[k - 1],
                     (here_p, (here_c + k) % ncomp))

    for load in loads[pieces + 1 :]:
        load.wait()

    def pair_dot(chip, c):
        rows2 = gathered[c, pl.ds(2 * chip, 2)].reshape(2 * rows, piece)
        return lax.dot_general(
            means[:, pl.ds(c * piece, piece)], rows2,
            (((1,), (1,)), ((), ())), preferred_element_type=jnp.float32,
        )

    def add_mean_squares(j, acc):
        x = means[:, pl.ds(pl.multiple_of(j * LANES, LANES), LANES)].astype(jnp.float32)
        return acc + x * x

    sq = lax.fori_loop(
        0, width // LANES, add_mean_squares, jnp.zeros((owned, LANES), jnp.float32)
    )
    mm = jnp.sum(sq, axis=1, keepdims=True)
    eye_k = lax.broadcasted_iota(jnp.int32, (owned, owned), 0) == lax.broadcasted_iota(
        jnp.int32, (owned, owned), 1
    )
    var = jnp.sum(jnp.where(eye_k, var_row[...], 0.0), axis=1, keepdims=True)
    logw = jnp.sum(jnp.where(eye_k, logw_row[...], 0.0), axis=1, keepdims=True)
    const = logw - 0.5 * width * jnp.log(2.0 * math.pi * var)
    two_var = 2.0 * var

    def named(s, b):
        number = (here_c * 2 + b).astype(jnp.float32)
        hit = aux[s, 0:1, :] == number
        for j in range(1, ncand):
            hit = hit | (aux[s, j : j + 1, :] == number)
        return hit

    def finish(s, g):
        xx = aux[s, ncand : ncand + 1, :]
        lp = const - (xx - 2.0 * g + mm) / two_var
        logp[s] = lp
        tops, totals = [], []
        for b in range(2):
            half = lp[b * block : (b + 1) * block]
            top = jnp.max(half, axis=0, keepdims=True)
            hit = named(s, b)
            part_sum = jnp.sum(jnp.exp(half - top), axis=0, keepdims=True)
            tops.append(jnp.where(hit, top, LOW))
            totals.append(jnp.where(hit, part_sum, 0.0))
        top = jnp.maximum(tops[0], tops[1])
        stats[here_c, s, 0:1, :] = top
        stats[here_c, s, 1:2, :] = totals[0] * jnp.exp(tops[0] - top) + totals[1] * jnp.exp(
            tops[1] - top
        )
        for k in range(1, ncomp):
            send(stats.at[here_c, s], stats.at[here_c, s], st_send.at[k - 1, s],
                 st_recv.at[k - 1, s], (here_p, (here_c + k) % ncomp))

    def add_pair(chip, c):
        g = pair_dot(chip, c)
        if c:
            g = partial[chip] + g
        if c < pieces - 1:
            partial[chip] = g
        else:
            for j in range(2):
                finish(2 * chip + j, g[:, j * rows : (j + 1) * rows])

    def take_forwarded(c):
        for k in range(1, ny):
            chip = (y + ny - k) % ny
            arrived(part(chip * 2 + other_core, c), fwd_send.at[k - 1, c], fwd_recv.at[k - 1, c])
            add_pair(chip, c)

    own = 0
    for c in range(pieces):
        for k in range(1, ny):
            slot = ((y + ny - k) % ny) * 2 + core
            arrived(part(slot, c), y_send.at[k - 1, c], y_recv.at[k - 1, c])
            send(part(slot, c), part(slot, c), fwd_send.at[k - 1, c], fwd_recv.at[k - 1, c],
                 (here_p, sibling))
        if c + ahead < pieces:
            send_y(c + ahead)
        for n in range(ahead + 2 * c, min(pieces, ahead + 2 * c + 2)):
            send_sibling(n)
        if c == 0:
            for k in range(1, ncomp):
                arrived(aux.at[(here_c + ncomp - k) % ncomp], aux_send.at[k - 1],
                        aux_recv.at[k - 1])
        for _ in range(2):
            if own < pieces:
                arrived(part(sibling, own), sib_send.at[own], sib_recv.at[own])
                add_pair(y, own)
                own += 1
        if c:
            take_forwarded(c - 1)
    take_forwarded(pieces - 1)

    for k in range(1, ncomp):
        owner = (here_c + ncomp - k) % ncomp
        for s in range(ncomp):
            arrived(stats.at[owner, s], st_send.at[k - 1, s], st_recv.at[k - 1, s])

    count_sum = [jnp.zeros((block, rows), jnp.float32) for _ in range(2)]
    sq_sum = [jnp.zeros((block, rows), jnp.float32) for _ in range(2)]
    for s in range(ncomp):
        lanes = slice(s * rows, (s + 1) * rows)
        tops = [stats[o, s, 0:1, :] for o in range(ncomp)]
        top = functools.reduce(jnp.maximum, tops)
        weight = stats[0, s, 1:2, :] * jnp.exp(tops[0] - top)
        for o in range(1, ncomp):
            weight = weight + stats[o, s, 1:2, :] * jnp.exp(tops[o] - top)
        loglik = top + jnp.log(weight)
        logliks[s] = loglik
        xx = aux[s, ncand : ncand + 1, :]
        for b in range(2):
            resp = jnp.where(
                named(s, b), jnp.exp(logp[s, b * block : (b + 1) * block, :] - loglik), 0.0
            )
            resp16[b * block : (b + 1) * block, lanes] = resp.astype(jnp.bfloat16)
            count_sum[b] = count_sum[b] + resp
            sq_sum[b] = sq_sum[b] + resp * xx

    def make(c):
        data = gathered[c].reshape(ncomp * rows, piece)
        w = jnp.dot(resp16[...], data, preferred_element_type=jnp.float32)
        for g in range(ngroups):
            for n in range(4):
                lo, hi = n % 2, n // 2
                start = (g * 4 + n) * share
                wsend[c, lo + core * (hi - lo), hi + core * (lo - hi), g] = w[
                    start : start + share
                ].astype(jnp.bfloat16)
        send(wsend.at[c, 1 - bits[0]], land0.at[c], send0.at[c], recv0.at[c],
             (partners[0], here_c))

    def halve(c):
        mine, other = bits[1], 1 - bits[1]
        arrived(land0.at[c], send0.at[c], recv0.at[c])
        relay1[c] = (
            wsend[c, bits[0], other].astype(jnp.float32) + land0[c, other].astype(jnp.float32)
        ).astype(jnp.bfloat16)
        send(relay1.at[c], land1.at[c], send1.at[c], recv1.at[c], (partners[1], here_c))
        kept[c] = wsend[c, bits[0], mine].astype(jnp.float32) + land0[c, mine].astype(
            jnp.float32
        )

    def spread(c):
        arrived(land1.at[c], send1.at[c], recv1.at[c])
        both = kept[c] + land1[c].astype(jnp.float32)
        relay2[c] = both.astype(jnp.bfloat16)
        for k in range(1, ngroups):
            to = (group + k) % ngroups
            send(relay2.at[c, to], land2.at[k - 1, c], send2.at[k - 1, c], recv2.at[k - 1, c],
                 (to * 4 + here_p % 4, here_c))
        total[c] = both

    def share_sums():
        store(logliks.at[here_c], loglik_ref, 0)
        for b in range(2):
            cols = slice(b * block, (b + 1) * block)
            sums[0, 0:1, cols] = jnp.sum(count_sum[b].T, axis=0, keepdims=True)
            sums[0, 1:2, cols] = jnp.sum(sq_sum[b].T, axis=0, keepdims=True)
        for k in range(1, npts):
            send(sums.at[0], sums.at[k], sum_send.at[k - 1], sum_recv.at[k - 1],
                 ((here_p + k) % npts, here_c))

    def take_sums():
        for k in range(1, npts):
            arrived(sums.at[k], sum_send.at[k - 1], sum_recv.at[k - 1])
        both = sums[0]
        for k in range(1, npts):
            both = both + sums[k]
        both_sums[...] = both
        store(both_sums, sums_ref, 1)

    lag = 2
    for t in range(pieces + lag + 2):
        if t < pieces:
            make(t)
        if t == 1:
            share_sums()
        if lag <= t < pieces + lag:
            halve(t - lag)
        if lag < t <= pieces + lag:
            spread(t - lag - 1)
        if t == pieces:
            take_sums()
        if t >= lag + 2:
            c = t - lag - 2
            w = total[c, group]
            for k in range(1, ngroups):
                arrived(land2.at[k - 1, c], send2.at[k - 1, c], recv2.at[k - 1, c])
                w = w + land2[k - 1, c].astype(jnp.float32)
            wsum[c] = w
            store(wsum.at[c], wsum_ref.at[:, pl.ds(c * piece, piece)], 2 + c)

    for copy in stores:
        copy.wait()
    for copy in sends:
        copy.wait_send()


def update_kernel(
    npoints, ncomponents,
    loglik_in, wsum_in, sums_in, shares_ref, var_in,
    loglik_out, mean_out, newvar_out, newlogw_out,
    loglik, wsum_ref, sums_ref, mu_old, var_ref, mean_ref, newvar_ref, newlogw_ref,
    load_sem, out_sem,
):
    here_p = lax.axis_index("pts")
    pairs = [
        (sums_in, sums_ref), (var_in, var_ref), (wsum_in, wsum_ref),
        (shares_ref.at[here_p], mu_old), (loglik_in, loglik),
    ]
    loads = [
        pltpu.make_async_copy(src, dst, load_sem.at[i]) for i, (src, dst) in enumerate(pairs)
    ]
    for load in loads:
        load.start()
    share, width = wsum_ref.shape
    owned = sums_ref.shape[1]
    mine = lax.broadcasted_iota(jnp.int32, (share, owned), 1) == (
        lax.broadcasted_iota(jnp.int32, (share, owned), 0) + here_p * share
    )

    def column(row):
        return jnp.sum(jnp.where(mine, row, 0.0), axis=1, keepdims=True)

    for load in loads:
        load.wait()
    counts, sqsum = column(sums_ref[0:1, :]), column(sums_ref[1:2, :])
    var_old = column(var_ref[...])
    scale = 1.0 / (counts + 1.0)
    cross = jnp.zeros((share, LANES), jnp.float32)
    norm = jnp.zeros((share, LANES), jnp.float32)
    for j in range(width // LANES):
        cols = slice(j * LANES, (j + 1) * LANES)
        w = wsum_ref[:, cols]
        new = (w + mu_old[:, cols].astype(jnp.float32)) * scale
        mean_ref[:, cols] = new
        cross = cross + new * w
        norm = norm + new * new
    stores = [
        pltpu.make_async_copy(loglik, loglik_out, out_sem.at[0]),
        pltpu.make_async_copy(mean_ref, mean_out, out_sem.at[1]),
    ]
    for store in stores:
        store.start()
    cross = jnp.sum(cross, axis=1, keepdims=True)
    norm = jnp.sum(norm, axis=1, keepdims=True)
    resid = sqsum - 2.0 * cross + counts * norm + width * var_old
    new_var = resid / (width * (counts + 1.0))
    new_logw = jnp.log((counts + 1.0) / float(npoints + ncomponents))
    eye = lax.broadcasted_iota(jnp.int32, (share, share), 0) == lax.broadcasted_iota(
        jnp.int32, (share, share), 1
    )
    newvar_ref[...] = jnp.sum(jnp.where(eye, new_var, 0.0), axis=0, keepdims=True)
    newlogw_ref[...] = jnp.sum(jnp.where(eye, new_logw, 0.0), axis=0, keepdims=True)
    last = [
        pltpu.make_async_copy(newvar_ref, newvar_out, out_sem.at[2]),
        pltpu.make_async_copy(newlogw_ref, newlogw_out, out_sem.at[3]),
    ]
    for store in last:
        store.start()
    for store in stores + last:
        store.wait()


def on_device(ncomp, npts, points, candidates, means, variances, log_weights):
    rows, width = points.shape
    owned = means.shape[0]
    share = owned // npts
    ngroups = npts // 4
    pieces = 6
    ncand = candidates.shape[1]
    ny = ncomp // 2
    aux_rows = -(-(ncand + 1) // 8) * 8
    f32, bf16 = jnp.float32, jnp.bfloat16
    dma = pltpu.SemaphoreType.DMA
    anywhere = pl.BlockSpec(memory_space=pl.ANY)
    piece = width // pieces
    loglik, wsum, sums = pl.pallas_call(
        functools.partial(em_kernel, ncomp, npts, pieces),
        out_shape=(
            jax.ShapeDtypeStruct((1, rows), f32),
            jax.ShapeDtypeStruct((share, width), f32),
            jax.ShapeDtypeStruct((2, owned), f32),
        ),
        in_specs=[anywhere] * 5,
        out_specs=(anywhere,) * 3,
        scratch_shapes=[
            pltpu.VMEM((pieces, ncomp, rows, piece), bf16),
            pltpu.VMEM((owned, width), bf16),
            pltpu.VMEM((ncand, rows), jnp.int32),
            pltpu.VMEM((1, owned), f32),
            pltpu.VMEM((1, owned), f32),
            pltpu.VMEM((ncomp, aux_rows, rows), f32),
            pltpu.VMEM((ny, owned, 2 * rows), f32),
            pltpu.VMEM((ncomp, owned, rows), f32),
            pltpu.VMEM((ncomp, ncomp, 2, rows), f32),
            pltpu.VMEM((ncomp, 1, rows), f32),
            pltpu.VMEM((owned, ncomp * rows), bf16),
            pltpu.VMEM((npts, 2, owned), f32),
            pltpu.VMEM((pieces, 2, 2, ngroups, share, piece), bf16),
            pltpu.VMEM((pieces, 2, ngroups, share, piece), bf16),
            pltpu.VMEM((pieces, ngroups, share, piece), f32),
            pltpu.VMEM((pieces, ngroups, share, piece), bf16),
            pltpu.VMEM((pieces, ngroups, share, piece), bf16),
            pltpu.VMEM((pieces, ngroups, share, piece), f32),
            pltpu.VMEM((pieces, ngroups, share, piece), bf16),
            pltpu.VMEM((ngroups - 1, pieces, share, piece), bf16),
            pltpu.VMEM((pieces, share, piece), f32),
            pltpu.VMEM((2, owned), f32),
            dma((pieces + 4,)),
            dma((ny - 1, pieces)), dma((ny - 1, pieces)),
            dma((pieces,)), dma((pieces,)),
            dma((ny - 1, pieces)), dma((ny - 1, pieces)),
            dma((ncomp - 1,)), dma((ncomp - 1,)),
            dma((ncomp - 1, ncomp)), dma((ncomp - 1, ncomp)),
            dma((npts - 1,)), dma((npts - 1,)),
            dma((pieces,)), dma((pieces,)),
            dma((pieces,)), dma((pieces,)),
            dma((ngroups - 1, pieces)), dma((ngroups - 1, pieces)),
            dma((pieces + 2,)),
        ],
        compiler_params=pltpu.CompilerParams(
            collective_id=0, has_side_effects=True, vmem_limit_bytes=60 * 1024 * 1024
        ),
        name="em_step",
    )(
        points, candidates.T, means, variances.reshape(1, owned), log_weights.reshape(1, owned)
    )
    loglik, new_means, new_var, new_logw = pl.pallas_call(
        functools.partial(update_kernel, rows * ncomp * npts, owned * ncomp),
        out_shape=(
            jax.ShapeDtypeStruct((1, rows), f32),
            jax.ShapeDtypeStruct((share, width), f32),
            jax.ShapeDtypeStruct((1, share), f32),
            jax.ShapeDtypeStruct((1, share), f32),
        ),
        in_specs=[anywhere] * 5,
        out_specs=(anywhere,) * 4,
        scratch_shapes=[
            pltpu.VMEM((1, rows), f32),
            pltpu.VMEM((share, width), f32),
            pltpu.VMEM((2, owned), f32),
            pltpu.VMEM((share, width), bf16),
            pltpu.VMEM((1, owned), f32),
            pltpu.VMEM((share, width), f32),
            pltpu.VMEM((1, share), f32),
            pltpu.VMEM((1, share), f32),
            dma((5,)), dma((4,)),
        ],
        compiler_params=pltpu.CompilerParams(vmem_limit_bytes=60 * 1024 * 1024),
        name="update",
    )(loglik, wsum, sums, means.reshape(npts, share, width), variances.reshape(1, owned))
    return (
        loglik.reshape(rows),
        new_means.reshape(1, share, width),
        new_var,
        new_logw,
    )


def solution(mesh):
    return jax.shard_map(
        functools.partial(on_device, mesh.shape["comp"], mesh.shape["pts"]),
        mesh=mesh,
        in_specs=(
            P(("pts", "comp"), None),
            P(("pts", "comp"), None),
            P("comp", None),
            P("comp"),
            P("comp"),
        ),
        out_specs=(P(("pts", "comp")), P("comp", "pts", None), P("comp", "pts"), P("comp", "pts")),
        check_vma=False,
    )
```

```python
import functools
import math

import jax
import jax.numpy as jnp
from jax import lax
from jax.experimental import pallas as pl
from jax.experimental.pallas import tpu as pltpu
from jax.sharding import PartitionSpec as P

MESH = pl.DeviceIdType.MESH
LANES = 128
LOW = -3.0e38


def em_kernel(
    ncomp, npts, pieces,
    points_ref, cand_ref, means_ref, var_ref, logw_ref,
    loglik_ref, wsum_ref, sums_ref,
    gathered, means, cands, var_row, logw_row, aux, partial, logp, stats, logliks, resp16, sums,
    wsend, land0, kept, relay1, land1, total, relay2, land2, wsum, both_sums,
    load_sem, y_send, y_recv, sib_send, sib_recv, fwd_send, fwd_recv,
    aux_send, aux_recv, st_send, st_recv, sum_send, sum_recv,
    send0, recv0, send1, recv1, send2, recv2, out_sem,
):
    here_c, here_p = lax.axis_index("comp"), lax.axis_index("pts")
    ny, ngroups = ncomp // 2, npts // 4
    rows, width = points_ref.shape
    owned = means_ref.shape[0]
    block = owned // 2
    share = owned // npts
    piece = width // pieces
    ncand = cand_ref.shape[0]
    y, core = here_c // 2, here_c % 2
    other_core = 1 - core
    sibling = y * 2 + other_core
    group = here_p // 4
    bit0, bit1 = here_p % 2, (here_p // 2) % 2
    bits = (bit0 + other_core * (bit1 - bit0), bit1 + other_core * (bit0 - bit1))
    strides = (1 + other_core, 2 - other_core)
    partners = tuple(here_p + (1 - 2 * bit) * stride for bit, stride in zip(bits, strides))

    barrier = pltpu.get_barrier_semaphore()
    for k in range(1, ncomp):
        pl.semaphore_signal(
            barrier, inc=1, device_id=(here_p, (here_c + k) % ncomp), device_id_type=MESH
        )
    for k in range(1, npts):
        pl.semaphore_signal(
            barrier, inc=1, device_id=((here_p + k) % npts, here_c), device_id_type=MESH
        )

    loads = [
        pltpu.make_async_copy(src, dst, load_sem.at[i])
        for i, (src, dst) in enumerate(
            [(cand_ref, cands)]
            + [
                (points_ref.at[:, pl.ds(c * piece, piece)], gathered.at[c, here_c])
                for c in range(pieces)
            ]
            + [(means_ref, means), (var_ref, var_row), (logw_ref, logw_row)]
        )
    ]
    for load in loads:
        load.start()

    for load in loads[: pieces + 1]:
        load.wait()

    def add_point_squares(c, acc):
        for j in range(piece // LANES):
            x = gathered[c, here_c, :, j * LANES : (j + 1) * LANES].astype(jnp.float32)
            acc = acc + x * x
        return acc

    sq = lax.fori_loop(0, pieces, add_point_squares, jnp.zeros((rows, LANES), jnp.float32))
    xx_row = jnp.sum(sq.T, axis=0, keepdims=True)
    aux[here_c] = jnp.concatenate(
        [cands[...].astype(jnp.float32), xx_row]
        + [jnp.zeros((aux.shape[1] - ncand - 1, rows), jnp.float32)],
        axis=0,
    )
    pl.semaphore_wait(barrier, ncomp + npts - 2)

    sends, stores = [], []

    def store(src, dst, i):
        copy = pltpu.make_async_copy(src, dst, out_sem.at[i])
        copy.start()
        stores.append(copy)

    def send(src, dst, s_sem, r_sem, device):
        copy = pltpu.make_async_remote_copy(
            src_ref=src, dst_ref=dst, send_sem=s_sem, recv_sem=r_sem,
            device_id=device, device_id_type=MESH,
        )
        copy.start()
        sends.append(copy)

    def arrived(dst, s_sem, r_sem):
        pltpu.make_async_remote_copy(
            src_ref=dst, dst_ref=dst, send_sem=s_sem, recv_sem=r_sem,
            device_id=(here_p, sibling), device_id_type=MESH,
        ).wait_recv()

    def part(slot, c):
        return gathered.at[c, slot]

    def send_y(c):
        for k in range(1, ny):
            send(part(here_c, c), part(here_c, c), y_send.at[k - 1, c], y_recv.at[k - 1, c],
                 (here_p, ((y + k) % ny) * 2 + core))

    def send_sibling(c):
        send(part(here_c, c), part(here_c, c), sib_send.at[c], sib_recv.at[c], (here_p, sibling))

    ahead = 2
    for c in range(ahead):
        send_y(c)
        send_sibling(c)
        if c == 0:
            for k in range(1, ncomp):
                send(aux.at[here_c], aux.at[here_c], aux_send.at[k - 1], aux_recv.at[k - 1],
                     (here_p, (here_c + k) % ncomp))

    for load in loads[pieces + 1 :]:
        load.wait()

    def pair_dot(chip, c):
        rows2 = gathered[c, pl.ds(2 * chip, 2)].reshape(2 * rows, piece)
        return lax.dot_general(
            means[:, pl.ds(c * piece, piece)], rows2,
            (((1,), (1,)), ((), ())), preferred_element_type=jnp.float32,
        )

    def add_mean_squares(j, acc):
        x = means[:, pl.ds(pl.multiple_of(j * LANES, LANES), LANES)].astype(jnp.float32)
        return acc + x * x

    sq = lax.fori_loop(
        0, width // LANES, add_mean_squares, jnp.zeros((owned, LANES), jnp.float32)
    )
    mm = jnp.sum(sq, axis=1, keepdims=True)
    eye_k = lax.broadcasted_iota(jnp.int32, (owned, owned), 0) == lax.broadcasted_iota(
        jnp.int32, (owned, owned), 1
    )
    var = jnp.sum(jnp.where(eye_k, var_row[...], 0.0), axis=1, keepdims=True)
    logw = jnp.sum(jnp.where(eye_k, logw_row[...], 0.0), axis=1, keepdims=True)
    const = logw - 0.5 * width * jnp.log(2.0 * math.pi * var)
    two_var = 2.0 * var

    def named(s, b):
        number = (here_c * 2 + b).astype(jnp.float32)
        hit = aux[s, 0:1, :] == number
        for j in range(1, ncand):
            hit = hit | (aux[s, j : j + 1, :] == number)
        return hit

    def finish(s, g):
        xx = aux[s, ncand : ncand + 1, :]
        lp = const - (xx - 2.0 * g + mm) / two_var
        logp[s] = lp
        tops, totals = [], []
        for b in range(2):
            half = lp[b * block : (b + 1) * block]
            top = jnp.max(half, axis=0, keepdims=True)
            hit = named(s, b)
            part_sum = jnp.sum(jnp.exp(half - top), axis=0, keepdims=True)
            tops.append(jnp.where(hit, top, LOW))
            totals.append(jnp.where(hit, part_sum, 0.0))
        top = jnp.maximum(tops[0], tops[1])
        stats[here_c, s, 0:1, :] = top
        stats[here_c, s, 1:2, :] = totals[0] * jnp.exp(tops[0] - top) + totals[1] * jnp.exp(
            tops[1] - top
        )
        for k in range(1, ncomp):
            send(stats.at[here_c, s], stats.at[here_c, s], st_send.at[k - 1, s],
                 st_recv.at[k - 1, s], (here_p, (here_c + k) % ncomp))

    def add_pair(chip, c):
        g = pair_dot(chip, c)
        if c:
            g = partial[chip] + g
        if c < pieces - 1:
            partial[chip] = g
        else:
            for j in range(2):
                finish(2 * chip + j, g[:, j * rows : (j + 1) * rows])

    def take_forwarded(c):
        for k in range(1, ny):
            chip = (y + ny - k) % ny
            arrived(part(chip * 2 + other_core, c), fwd_send.at[k - 1, c], fwd_recv.at[k - 1, c])
            add_pair(chip, c)

    own = 0
    for c in range(pieces):
        for k in range(1, ny):
            slot = ((y + ny - k) % ny) * 2 + core
            arrived(part(slot, c), y_send.at[k - 1, c], y_recv.at[k - 1, c])
            send(part(slot, c), part(slot, c), fwd_send.at[k - 1, c], fwd_recv.at[k - 1, c],
                 (here_p, sibling))
        if c + ahead < pieces:
            send_y(c + ahead)
        for n in range(ahead + 2 * c, min(pieces, ahead + 2 * c + 2)):
            send_sibling(n)
        if c == 0:
            for k in range(1, ncomp):
                arrived(aux.at[(here_c + ncomp - k) % ncomp], aux_send.at[k - 1],
                        aux_recv.at[k - 1])
        for _ in range(2):
            if own < pieces:
                arrived(part(sibling, own), sib_send.at[own], sib_recv.at[own])
                add_pair(y, own)
                own += 1
        if c:
            take_forwarded(c - 1)
    take_forwarded(pieces - 1)

    for k in range(1, ncomp):
        owner = (here_c + ncomp - k) % ncomp
        for s in range(ncomp):
            arrived(stats.at[owner, s], st_send.at[k - 1, s], st_recv.at[k - 1, s])

    count_sum = [jnp.zeros((block, rows), jnp.float32) for _ in range(2)]
    sq_sum = [jnp.zeros((block, rows), jnp.float32) for _ in range(2)]
    for s in range(ncomp):
        lanes = slice(s * rows, (s + 1) * rows)
        tops = [stats[o, s, 0:1, :] for o in range(ncomp)]
        top = functools.reduce(jnp.maximum, tops)
        weight = stats[0, s, 1:2, :] * jnp.exp(tops[0] - top)
        for o in range(1, ncomp):
            weight = weight + stats[o, s, 1:2, :] * jnp.exp(tops[o] - top)
        loglik = top + jnp.log(weight)
        logliks[s] = loglik
        xx = aux[s, ncand : ncand + 1, :]
        for b in range(2):
            resp = jnp.where(
                named(s, b), jnp.exp(logp[s, b * block : (b + 1) * block, :] - loglik), 0.0
            )
            resp16[b * block : (b + 1) * block, lanes] = resp.astype(jnp.bfloat16)
            count_sum[b] = count_sum[b] + resp
            sq_sum[b] = sq_sum[b] + resp * xx

    def make(c):
        data = gathered[c].reshape(ncomp * rows, piece)
        w = jnp.dot(resp16[...], data, preferred_element_type=jnp.float32)
        for g in range(ngroups):
            for n in range(4):
                lo, hi = n % 2, n // 2
                start = (g * 4 + n) * share
                wsend[c, lo + other_core * (hi - lo), hi + other_core * (lo - hi), g] = w[
                    start : start + share
                ].astype(jnp.bfloat16)
        send(wsend.at[c, 1 - bits[0]], land0.at[c], send0.at[c], recv0.at[c],
             (partners[0], here_c))

    def halve(c):
        mine, other = bits[1], 1 - bits[1]
        arrived(land0.at[c], send0.at[c], recv0.at[c])
        relay1[c] = (
            wsend[c, bits[0], other].astype(jnp.float32) + land0[c, other].astype(jnp.float32)
        ).astype(jnp.bfloat16)
        send(relay1.at[c], land1.at[c], send1.at[c], recv1.at[c], (partners[1], here_c))
        kept[c] = wsend[c, bits[0], mine].astype(jnp.float32) + land0[c, mine].astype(
            jnp.float32
        )

    def spread(c):
        arrived(land1.at[c], send1.at[c], recv1.at[c])
        both = kept[c] + land1[c].astype(jnp.float32)
        relay2[c] = both.astype(jnp.bfloat16)
        for k in range(1, ngroups):
            to = (group + k) % ngroups
            send(relay2.at[c, to], land2.at[k - 1, c], send2.at[k - 1, c], recv2.at[k - 1, c],
                 (to * 4 + here_p % 4, here_c))
        total[c] = both

    def share_sums():
        store(logliks.at[here_c], loglik_ref, 0)
        for b in range(2):
            cols = slice(b * block, (b + 1) * block)
            sums[0, 0:1, cols] = jnp.sum(count_sum[b].T, axis=0, keepdims=True)
            sums[0, 1:2, cols] = jnp.sum(sq_sum[b].T, axis=0, keepdims=True)
        for k in range(1, npts):
            send(sums.at[0], sums.at[k], sum_send.at[k - 1], sum_recv.at[k - 1],
                 ((here_p + k) % npts, here_c))

    def take_sums():
        for k in range(1, npts):
            arrived(sums.at[k], sum_send.at[k - 1], sum_recv.at[k - 1])
        both = sums[0]
        for k in range(1, npts):
            both = both + sums[k]
        both_sums[...] = both
        store(both_sums, sums_ref, 1)

    lag = 2
    for t in range(pieces + lag + 2):
        if t < pieces:
            make(t)
        if t == 1:
            share_sums()
        if lag <= t < pieces + lag:
            halve(t - lag)
        if lag < t <= pieces + lag:
            spread(t - lag - 1)
        if t == pieces:
            take_sums()
        if t >= lag + 2:
            c = t - lag - 2
            w = total[c, group]
            for k in range(1, ngroups):
                arrived(land2.at[k - 1, c], send2.at[k - 1, c], recv2.at[k - 1, c])
                w = w + land2[k - 1, c].astype(jnp.float32)
            wsum[c] = w
            store(wsum.at[c], wsum_ref.at[:, pl.ds(c * piece, piece)], 2 + c)

    for copy in stores:
        copy.wait()
    for copy in sends:
        copy.wait_send()


def update_kernel(
    npoints, ncomponents,
    loglik_in, wsum_in, sums_in, shares_ref, var_in,
    loglik_out, mean_out, newvar_out, newlogw_out,
    loglik, wsum_ref, sums_ref, mu_old, var_ref, mean_ref, newvar_ref, newlogw_ref,
    load_sem, out_sem,
):
    here_p = lax.axis_index("pts")
    pairs = [
        (sums_in, sums_ref), (var_in, var_ref), (wsum_in, wsum_ref),
        (shares_ref.at[here_p], mu_old), (loglik_in, loglik),
    ]
    loads = [
        pltpu.make_async_copy(src, dst, load_sem.at[i]) for i, (src, dst) in enumerate(pairs)
    ]
    for load in loads:
        load.start()
    share, width = wsum_ref.shape
    owned = sums_ref.shape[1]
    mine = lax.broadcasted_iota(jnp.int32, (share, owned), 1) == (
        lax.broadcasted_iota(jnp.int32, (share, owned), 0) + here_p * share
    )

    def column(row):
        return jnp.sum(jnp.where(mine, row, 0.0), axis=1, keepdims=True)

    for load in loads:
        load.wait()
    counts, sqsum = column(sums_ref[0:1, :]), column(sums_ref[1:2, :])
    var_old = column(var_ref[...])
    scale = 1.0 / (counts + 1.0)
    cross = jnp.zeros((share, LANES), jnp.float32)
    norm = jnp.zeros((share, LANES), jnp.float32)
    for j in range(width // LANES):
        cols = slice(j * LANES, (j + 1) * LANES)
        w = wsum_ref[:, cols]
        new = (w + mu_old[:, cols].astype(jnp.float32)) * scale
        mean_ref[:, cols] = new
        cross = cross + new * w
        norm = norm + new * new
    stores = [
        pltpu.make_async_copy(loglik, loglik_out, out_sem.at[0]),
        pltpu.make_async_copy(mean_ref, mean_out, out_sem.at[1]),
    ]
    for store in stores:
        store.start()
    cross = jnp.sum(cross, axis=1, keepdims=True)
    norm = jnp.sum(norm, axis=1, keepdims=True)
    resid = sqsum - 2.0 * cross + counts * norm + width * var_old
    new_var = resid / (width * (counts + 1.0))
    new_logw = jnp.log((counts + 1.0) / float(npoints + ncomponents))
    eye = lax.broadcasted_iota(jnp.int32, (share, share), 0) == lax.broadcasted_iota(
        jnp.int32, (share, share), 1
    )
    newvar_ref[...] = jnp.sum(jnp.where(eye, new_var, 0.0), axis=0, keepdims=True)
    newlogw_ref[...] = jnp.sum(jnp.where(eye, new_logw, 0.0), axis=0, keepdims=True)
    last = [
        pltpu.make_async_copy(newvar_ref, newvar_out, out_sem.at[2]),
        pltpu.make_async_copy(newlogw_ref, newlogw_out, out_sem.at[3]),
    ]
    for store in last:
        store.start()
    for store in stores + last:
        store.wait()


def on_device(ncomp, npts, points, candidates, means, variances, log_weights):
    rows, width = points.shape
    owned = means.shape[0]
    share = owned // npts
    ngroups = npts // 4
    pieces = 6
    ncand = candidates.shape[1]
    ny = ncomp // 2
    aux_rows = -(-(ncand + 1) // 8) * 8
    f32, bf16 = jnp.float32, jnp.bfloat16
    dma = pltpu.SemaphoreType.DMA
    anywhere = pl.BlockSpec(memory_space=pl.ANY)
    piece = width // pieces
    loglik, wsum, sums = pl.pallas_call(
        functools.partial(em_kernel, ncomp, npts, pieces),
        out_shape=(
            jax.ShapeDtypeStruct((1, rows), f32),
            jax.ShapeDtypeStruct((share, width), f32),
            jax.ShapeDtypeStruct((2, owned), f32),
        ),
        in_specs=[anywhere] * 5,
        out_specs=(anywhere,) * 3,
        scratch_shapes=[
            pltpu.VMEM((pieces, ncomp, rows, piece), bf16),
            pltpu.VMEM((owned, width), bf16),
            pltpu.VMEM((ncand, rows), jnp.int32),
            pltpu.VMEM((1, owned), f32),
            pltpu.VMEM((1, owned), f32),
            pltpu.VMEM((ncomp, aux_rows, rows), f32),
            pltpu.VMEM((ny, owned, 2 * rows), f32),
            pltpu.VMEM((ncomp, owned, rows), f32),
            pltpu.VMEM((ncomp, ncomp, 2, rows), f32),
            pltpu.VMEM((ncomp, 1, rows), f32),
            pltpu.VMEM((owned, ncomp * rows), bf16),
            pltpu.VMEM((npts, 2, owned), f32),
            pltpu.VMEM((pieces, 2, 2, ngroups, share, piece), bf16),
            pltpu.VMEM((pieces, 2, ngroups, share, piece), bf16),
            pltpu.VMEM((pieces, ngroups, share, piece), f32),
            pltpu.VMEM((pieces, ngroups, share, piece), bf16),
            pltpu.VMEM((pieces, ngroups, share, piece), bf16),
            pltpu.VMEM((pieces, ngroups, share, piece), f32),
            pltpu.VMEM((pieces, ngroups, share, piece), bf16),
            pltpu.VMEM((ngroups - 1, pieces, share, piece), bf16),
            pltpu.VMEM((pieces, share, piece), f32),
            pltpu.VMEM((2, owned), f32),
            dma((pieces + 4,)),
            dma((ny - 1, pieces)), dma((ny - 1, pieces)),
            dma((pieces,)), dma((pieces,)),
            dma((ny - 1, pieces)), dma((ny - 1, pieces)),
            dma((ncomp - 1,)), dma((ncomp - 1,)),
            dma((ncomp - 1, ncomp)), dma((ncomp - 1, ncomp)),
            dma((npts - 1,)), dma((npts - 1,)),
            dma((pieces,)), dma((pieces,)),
            dma((pieces,)), dma((pieces,)),
            dma((ngroups - 1, pieces)), dma((ngroups - 1, pieces)),
            dma((pieces + 2,)),
        ],
        compiler_params=pltpu.CompilerParams(
            collective_id=0, has_side_effects=True, vmem_limit_bytes=60 * 1024 * 1024
        ),
        name="em_step",
    )(
        points, candidates.T, means, variances.reshape(1, owned), log_weights.reshape(1, owned)
    )
    loglik, new_means, new_var, new_logw = pl.pallas_call(
        functools.partial(update_kernel, rows * ncomp * npts, owned * ncomp),
        out_shape=(
            jax.ShapeDtypeStruct((1, rows), f32),
            jax.ShapeDtypeStruct((share, width), f32),
            jax.ShapeDtypeStruct((1, share), f32),
            jax.ShapeDtypeStruct((1, share), f32),
        ),
        in_specs=[anywhere] * 5,
        out_specs=(anywhere,) * 4,
        scratch_shapes=[
            pltpu.VMEM((1, rows), f32),
            pltpu.VMEM((share, width), f32),
            pltpu.VMEM((2, owned), f32),
            pltpu.VMEM((share, width), bf16),
            pltpu.VMEM((1, owned), f32),
            pltpu.VMEM((share, width), f32),
            pltpu.VMEM((1, share), f32),
            pltpu.VMEM((1, share), f32),
            dma((5,)), dma((4,)),
        ],
        compiler_params=pltpu.CompilerParams(vmem_limit_bytes=60 * 1024 * 1024),
        name="update",
    )(loglik, wsum, sums, means.reshape(npts, share, width), variances.reshape(1, owned))
    return (
        loglik.reshape(rows),
        new_means.reshape(1, share, width),
        new_var,
        new_logw,
    )


def solution(mesh):
    return jax.shard_map(
        functools.partial(on_device, mesh.shape["comp"], mesh.shape["pts"]),
        mesh=mesh,
        in_specs=(
            P(("pts", "comp"), None),
            P(("pts", "comp"), None),
            P("comp", None),
            P("comp"),
            P("comp"),
        ),
        out_specs=(P(("pts", "comp")), P("comp", "pts", None), P("comp", "pts"), P("comp", "pts")),
        check_vma=False,
    )
```
